32 devices in a mesh: patch: 4 (over z), uly: 2 (over y), rep: 4 (over x, core).
Axes of the slice: x: 2, y: 2, z: 4, core: 2. Of those that a mesh axis runs over, the one named last changes fastest.
Arguments:
- queries: bfloat16 [512, 3072], P(('rep', 'patch', 'uly')), parts along dimension 0, may hold values from -130 to 130
- stale_kv: bfloat16 [512, 2, 3072], P('rep', None, 'uly'), parts along dimension 0, may hold values from -10 to 10
- codes: int32 [512, 2, 3072], P(('rep', 'patch', 'uly')), parts along dimension 0, may hold values from -127 to 127
- exps: int32 [512, 2, 24], P(('rep', 'patch', 'uly')), parts along dimension 0, may hold values from -10 to -6
Outputs:
- mixed: bfloat16 [512, 3072], P(('rep', 'patch', 'uly')), parts along dimension 0
The draws below stay inside these ranges and needn't reach their ends.
There are 4 independent parts, one for each index of `rep`. The reference program is written for one: setup_inputs(seed, part) draws one part's arguments, and reference() takes and returns one part's arrays. A program takes and returns all parts, laid end to end along the dimension named above; each array names one. Nothing has to cross between parts.
All inputs are finite; a program needn't handle non-finite values.
Results may differ from the reference program's by a relative error of at most 0.0076.
Values may be sent and summed in bfloat16 or wider, within the bound.
No kernel may reach another device: no remote copies, remote signals or barrier semaphores. Data moves between devices by JAX's collectives and lax.ppermute only.
A program may use at most 128 MiB of HBM per device.

```python
import math
import jax
import jax.numpy as jnp
from jax import lax

HEADS = 24
HEAD_DIM = 128
D = 3072
SCALE_BLOCK = 128
TOKENS = 128


def stale_base(key):
    return jnp.clip(jax.random.normal(key, (TOKENS, 2, D), jnp.float32), -5.0, 5.0)


def draw_stale_kv(key, part):
    base = stale_base(key)
    return base.astype(jnp.bfloat16)


def draw_queries(key, part):
    key = jax.random.fold_in(key, 7)
    values = 2.0 * jnp.clip(jax.random.normal(key, (TOKENS, D), jnp.float32), -6.0, 6.0)
    return values.astype(jnp.bfloat16)


def set_ends(array, own_key, low, top_value):
    dims = array.shape
    index_at = [jax.random.randint(jax.random.fold_in(own_key, axis), (), 0, dims[axis]) for axis in range(len(dims))]
    array = array.at[tuple(index_at)].set(low)
    longest = dims.index(max(dims))
    index_at[longest] = (index_at[longest] + 1) % dims[longest]
    return array.at[tuple(index_at)].set(top_value)


def setup_inputs(seed: int = 0, part: int = 0) -> dict:
    streams_of = jax.random.split(jax.random.key(seed), 5)
    own_keys = jax.random.split(jax.random.fold_in(streams_of[4], part), 5)
    queries = draw_queries(jax.random.fold_in(jax.random.fold_in(streams_of[4], part), 71), part)
    stale_kv = draw_stale_kv(jax.random.fold_in(jax.random.fold_in(streams_of[4], part), 71), part)
    codes = set_ends(jax.random.randint(own_keys[2], (TOKENS, 2, D), -127, 128), jax.random.fold_in(own_keys[2], 1), -127, 127).astype(jnp.int32)
    exps = set_ends(jax.random.randint(own_keys[3], (TOKENS, 2, D // SCALE_BLOCK), -10, -5), jax.random.fold_in(own_keys[3], 1), -10, (-5) - 1).astype(jnp.int32)
    return {"queries": queries, "stale_kv": stale_kv, "codes": codes, "exps": exps}


def decode(codes, exps):
    num_rows = codes.shape[0]
    num_blocks = exps.shape[2]
    scaled = codes.astype(jnp.float32).reshape(num_rows, 2, num_blocks, SCALE_BLOCK) * jnp.exp2(exps.astype(jnp.float32))[..., None]
    return scaled.reshape(num_rows, 2, num_blocks * SCALE_BLOCK).astype(jnp.bfloat16)

def reference(queries, stale_kv, codes, exps):
    residual = decode(codes, exps)
    keys_values = (stale_kv.astype(jnp.float32) + residual.astype(jnp.float32)).astype(jnp.bfloat16)
    query_heads = queries.reshape(TOKENS, HEADS, HEAD_DIM).transpose(1, 0, 2)
    key_heads = keys_values[:, 0].reshape(TOKENS, HEADS, HEAD_DIM).transpose(1, 0, 2)
    value_heads = keys_values[:, 1].reshape(TOKENS, HEADS, HEAD_DIM).transpose(1, 0, 2)
    factor = 1.0 / math.sqrt(HEAD_DIM)

    def one_head(operands):
        query_head, key_head, value_head = operands
        scores = jnp.dot(query_head, key_head.T, preferred_element_type=jnp.float32) * factor
        row_max = lax.optimization_barrier(jnp.max(scores, axis=1, keepdims=True))
        weights = jnp.exp(scores - row_max)
        totals = lax.optimization_barrier(jnp.sum(weights, axis=1, keepdims=True))
        return jnp.dot(weights.astype(jnp.bfloat16), value_head, preferred_element_type=jnp.float32) / totals
    attended = lax.map(one_head, (query_heads, key_heads, value_heads))
    return attended.transpose(1, 0, 2).reshape(TOKENS, D).astype(jnp.bfloat16)
```

```python
import functools
import math

import jax
import jax.numpy as jnp
from jax import lax
from jax.experimental import pallas as pl
from jax.sharding import PartitionSpec as P

HEAD_DIM = 128
SCALE_BLOCK = 128


def decode(codes, exps):
    num_rows = codes.shape[0]
    num_blocks = exps.shape[2]
    scaled = (
        codes.astype(jnp.float32).reshape(num_rows, 2, num_blocks, SCALE_BLOCK)
        * jnp.exp2(exps.astype(jnp.float32))[..., None]
    )
    return scaled.reshape(num_rows, 2, num_blocks * SCALE_BLOCK).astype(jnp.bfloat16)


def refresh(stale_part, resid_part):
    return (stale_part.astype(jnp.float32) + resid_part.astype(jnp.float32)).astype(jnp.bfloat16)


def column_block(rows, head):
    return rows[:, head * HEAD_DIM : (head + 1) * HEAD_DIM]


def head_scores(query_rows, key_rows, head):
    scores = lax.dot_general(
        column_block(query_rows, head),
        column_block(key_rows, head),
        (((1,), (1,)), ((), ())),
        preferred_element_type=jnp.float32,
    )
    return scores * (1.0 / math.sqrt(HEAD_DIM))


def weigh_values(weights, value_rows, head):
    return jnp.dot(
        weights.astype(jnp.bfloat16),
        column_block(value_rows, head),
        preferred_element_type=jnp.float32,
    )


def attend_whole(query_rows, kv_rows):
    head_count = query_rows.shape[1] // HEAD_DIM
    key_rows = kv_rows[:, 0]
    value_rows = kv_rows[:, 1]
    outputs = []
    for head in range(head_count):
        scores = head_scores(query_rows, key_rows, head)
        row_max = jnp.max(scores, axis=1, keepdims=True)
        weights = jnp.exp(scores - row_max)
        totals = jnp.sum(weights, axis=1, keepdims=True)
        outputs.append(weigh_values(weights, value_rows, head) / totals)
    return jnp.concatenate(outputs, axis=1).astype(jnp.bfloat16)


def attend_gathered(queries, stale_kv, codes, exps):
    residual = decode(codes, exps)
    query_rows = lax.all_to_all(queries, "uly", split_axis=1, concat_axis=0, tiled=True)
    gathered = lax.all_gather(residual, "patch", axis=0, tiled=True)
    patch_count = lax.axis_size("patch")
    blocked = gathered.reshape(patch_count, residual.shape[0], 2, residual.shape[2])
    spread = lax.all_to_all(blocked, "uly", split_axis=3, concat_axis=1, tiled=True)
    all_resid = spread.reshape(stale_kv.shape)
    result = attend_whole(query_rows, refresh(stale_kv, all_resid))
    return lax.all_to_all(result, "uly", split_axis=0, concat_axis=1, tiled=True)


def pack_kernel(queries_ref, codes_ref, exps_ref, packed_ref, *, patch_count, uly_count):
    width = packed_ref.shape[2]
    rows = queries_ref.shape[0]
    for patch in range(patch_count):
        for uly in range(uly_count):
            dest = patch * uly_count + uly
            start = (uly * patch_count + patch) * width
            packed_ref[dest, 0:rows, :] = queries_ref[:, start : start + width]
    for kind in range(2):
        scale = jnp.exp2(exps_ref[:, kind, :].astype(jnp.float32))
        for patch in range(patch_count):
            for uly in range(uly_count):
                dest = patch * uly_count + uly
                start = (uly * patch_count + patch) * width
                for offset in range(0, width, SCALE_BLOCK):
                    block = (start + offset) // SCALE_BLOCK
                    values = codes_ref[:, kind, start + offset : start + offset + SCALE_BLOCK].astype(jnp.float32)
                    decoded = values * scale[:, block : block + 1]
                    packed_ref[dest, (kind + 1) * rows : (kind + 2) * rows, offset : offset + SCALE_BLOCK] = decoded.astype(
                        jnp.bfloat16
                    )


def attend_kernel(blocks_ref, stale_ref, mixed_ref):
    sources, rows, width = mixed_ref.shape
    tokens = sources * rows

    def received(kind):
        return blocks_ref[:, kind * rows : (kind + 1) * rows, :].reshape(tokens, width)

    query_rows = received(0)
    key_rows = refresh(stale_ref[0], received(1))
    value_rows = refresh(stale_ref[1], received(2))
    for head in range(width // HEAD_DIM):
        scores = head_scores(query_rows, key_rows, head)
        weights = jnp.exp(scores - jnp.max(scores, axis=1, keepdims=True))
        totals = jnp.sum(weights, axis=1, keepdims=True)
        result = weigh_values(weights, value_rows, head) / totals
        mixed_ref[:, :, head * HEAD_DIM : (head + 1) * HEAD_DIM] = result.astype(jnp.bfloat16).reshape(sources, rows, HEAD_DIM)


def attend_split_heads(queries, stale_kv, codes, exps):
    patch_count = lax.axis_size("patch")
    uly_count = lax.axis_size("uly")
    peers = patch_count * uly_count
    rows, model_width = queries.shape
    tokens = stale_kv.shape[0]
    width = model_width // peers
    both = ("patch", "uly")
    packed = pl.pallas_call(
        functools.partial(pack_kernel, patch_count=patch_count, uly_count=uly_count),
        out_shape=jax.ShapeDtypeStruct((peers, 3 * rows, width), jnp.bfloat16),
    )(queries, codes, exps)
    blocks = lax.all_to_all(packed, both, split_axis=0, concat_axis=0, tiled=True)
    own_stale = lax.dynamic_slice(stale_kv, (0, 0, lax.axis_index("patch") * width), (tokens, 2, width))
    own_stale = jnp.swapaxes(own_stale, 0, 1)
    mixed = pl.pallas_call(
        attend_kernel,
        out_shape=jax.ShapeDtypeStruct((peers, rows, width), jnp.bfloat16),
    )(blocks, own_stale)
    back = lax.all_to_all(mixed, both, split_axis=0, concat_axis=0, tiled=True)
    return jnp.concatenate(
        [back[patch * uly_count + uly] for uly in range(uly_count) for patch in range(patch_count)], axis=1
    )


def on_device(queries, stale_kv, codes, exps):
    own_heads = stale_kv.shape[2] // HEAD_DIM
    if own_heads % lax.axis_size("patch") == 0:
        return attend_split_heads(queries, stale_kv, codes, exps)
    return attend_gathered(queries, stale_kv, codes, exps)


def solution(mesh):
    return jax.shard_map(
        on_device,
        mesh=mesh,
        in_specs=(
            P(("rep", "patch", "uly"), None),
            P("rep", None, "uly"),
            P(("rep", "patch", "uly"), None, None),
            P(("rep", "patch", "uly"), None, None),
        ),
        out_specs=P(("rep", "patch", "uly"), None),
        check_vma=False,
    )
```

```python
import functools
import math

import jax
import jax.numpy as jnp
from jax import lax
from jax.experimental import pallas as pl
from jax.experimental.pallas import tpu as pltpu
from jax.sharding import PartitionSpec as P

HEAD_DIM = 128
SCALE_BLOCK = 128
CODE_CHUNKS = 4
KERNEL_VMEM = 8 << 20
PACK_VMEM = 8 << 20


def decode(codes, exps):
    num_rows = codes.shape[0]
    num_blocks = exps.shape[2]
    scaled = (
        codes.astype(jnp.float32).reshape(num_rows, 2, num_blocks, SCALE_BLOCK)
        * jnp.exp2(exps.astype(jnp.float32))[..., None]
    )
    return scaled.reshape(num_rows, 2, num_blocks * SCALE_BLOCK).astype(jnp.bfloat16)


def refresh(stale_part, resid_part):
    return (stale_part.astype(jnp.float32) + resid_part.astype(jnp.float32)).astype(jnp.bfloat16)


def column_block(rows, head):
    return rows[:, head * HEAD_DIM : (head + 1) * HEAD_DIM]


def head_scores(query_rows, key_rows, head):
    scores = lax.dot_general(
        column_block(query_rows, head),
        column_block(key_rows, head),
        (((1,), (1,)), ((), ())),
        preferred_element_type=jnp.float32,
    )
    return scores * (1.0 / math.sqrt(HEAD_DIM))


def weigh_values(weights, value_rows, head):
    return jnp.dot(
        weights.astype(jnp.bfloat16),
        column_block(value_rows, head),
        preferred_element_type=jnp.float32,
    )


def attend_whole(query_rows, kv_rows):
    head_count = query_rows.shape[1] // HEAD_DIM
    key_rows = kv_rows[:, 0]
    value_rows = kv_rows[:, 1]
    outputs = []
    for head in range(head_count):
        scores = head_scores(query_rows, key_rows, head)
        row_max = jnp.max(scores, axis=1, keepdims=True)
        weights = jnp.exp(scores - row_max)
        totals = jnp.sum(weights, axis=1, keepdims=True)
        outputs.append(weigh_values(weights, value_rows, head) / totals)
    return jnp.concatenate(outputs, axis=1).astype(jnp.bfloat16)


def attend_gathered(queries, stale_kv, codes, exps):
    residual = decode(codes, exps)
    query_rows = lax.all_to_all(queries, "uly", split_axis=1, concat_axis=0, tiled=True)
    gathered = lax.all_gather(residual, "patch", axis=0, tiled=True)
    patch_count = lax.axis_size("patch")
    blocked = gathered.reshape(patch_count, residual.shape[0], 2, residual.shape[2])
    spread = lax.all_to_all(blocked, "uly", split_axis=3, concat_axis=1, tiled=True)
    all_resid = spread.reshape(stale_kv.shape)
    result = attend_whole(query_rows, refresh(stale_kv, all_resid))
    return lax.all_to_all(result, "uly", split_axis=0, concat_axis=1, tiled=True)


def home_column(peer, patch_count, uly_count, width):
    return ((peer % uly_count) * patch_count + peer // uly_count) * width


def pack_kernel(queries_hbm, codes_hbm, exps_hbm, packed_ref, queries_ref, codes_ref, exps_ref, sems, *, patch_count, uly_count):
    width = packed_ref.shape[2]
    rows = queries_ref.shape[0]
    peers = patch_count * uly_count
    fetch_exps = pltpu.make_async_copy(exps_hbm, exps_ref, sems.at[0])
    fetch_exps.start()
    fetch_codes = []
    half = codes_ref.shape[2] // CODE_CHUNKS
    for part in range(CODE_CHUNKS):
        columns = pl.ds(part * half, half)
        copies = [
            pltpu.make_async_copy(codes_hbm.at[:, kind, columns], codes_ref.at[kind, :, columns], sems.at[2 + 2 * part + kind])
            for kind in range(2)
        ]
        for copy in copies:
            copy.start()
        fetch_codes.append(copies)
    fetch_queries = pltpu.make_async_copy(queries_hbm, queries_ref, sems.at[1])
    fetch_queries.start()

    fetch_exps.wait()
    scales = [jnp.exp2(exps_ref[:, kind, :].astype(jnp.float32)) for kind in range(2)]
    ready = 0
    for peer in sorted(range(peers), key=lambda peer: home_column(peer, patch_count, uly_count, width)):
        start = home_column(peer, patch_count, uly_count, width)
        while ready * half < start + width:
            for copy in fetch_codes[ready]:
                copy.wait()
            ready += 1
        for kind in range(2):
            for offset in range(0, width, SCALE_BLOCK):
                block = (start + offset) // SCALE_BLOCK
                values = codes_ref[kind, :, start + offset : start + offset + SCALE_BLOCK].astype(jnp.float32)
                decoded = values * scales[kind][:, block : block + 1]
                packed_ref[peer, (kind + 1) * rows : (kind + 2) * rows, offset : offset + SCALE_BLOCK] = decoded.astype(
                    jnp.bfloat16
                )
    fetch_queries.wait()
    for peer in range(peers):
        start = home_column(peer, patch_count, uly_count, width)
        packed_ref[peer, 0:rows, :] = queries_ref[:, start : start + width]


def pack(queries, codes, exps, patch_count, uly_count):
    rows, model_width = queries.shape
    peers = patch_count * uly_count
    return pl.pallas_call(
        functools.partial(pack_kernel, patch_count=patch_count, uly_count=uly_count),
        out_shape=jax.ShapeDtypeStruct((peers, 3 * rows, model_width // peers), jnp.bfloat16),
        in_specs=[pl.BlockSpec(memory_space=pltpu.HBM)] * 3,
        out_specs=pl.BlockSpec(memory_space=pltpu.VMEM),
        scratch_shapes=[
            pltpu.VMEM(queries.shape, queries.dtype),
            pltpu.VMEM((2, rows, model_width), codes.dtype),
            pltpu.VMEM(exps.shape, exps.dtype),
            pltpu.SemaphoreType.DMA((2 + 2 * CODE_CHUNKS,)),
        ],
        compiler_params=pltpu.CompilerParams(vmem_limit_bytes=PACK_VMEM),
    )(*(pltpu.with_memory_space_constraint(each, pltpu.HBM) for each in (queries, codes, exps)))


def attend_kernel(blocks_ref, stale_ref, mixed_ref):
    sources, rows, width = mixed_ref.shape
    tokens = sources * rows
    heads = range(width // HEAD_DIM)

    def received(kind):
        return blocks_ref[:, kind * rows : (kind + 1) * rows, :].reshape(tokens, width)

    query_rows = received(0)
    key_rows = refresh(stale_ref[0], received(1))
    scores = [head_scores(query_rows, key_rows, head) for head in heads]
    value_rows = refresh(stale_ref[1], received(2))
    weights = [jnp.exp(each - jnp.max(each, axis=1, keepdims=True)) for each in scores]
    sums = [weigh_values(weights[head], value_rows, head) for head in heads]
    for head in heads:
        result = sums[head] / jnp.sum(weights[head], axis=1, keepdims=True)
        mixed_ref[:, :, head * HEAD_DIM : (head + 1) * HEAD_DIM] = result.astype(jnp.bfloat16).reshape(sources, rows, HEAD_DIM)


def attend(blocks, own_stale):
    peers, packed_rows, width = blocks.shape
    return pl.pallas_call(
        attend_kernel,
        out_shape=jax.ShapeDtypeStruct((peers, packed_rows // 3, width), jnp.bfloat16),
        in_specs=[pl.BlockSpec(memory_space=pltpu.VMEM)] * 2,
        out_specs=pl.BlockSpec(memory_space=pltpu.VMEM),
        compiler_params=pltpu.CompilerParams(vmem_limit_bytes=KERNEL_VMEM),
    )(blocks, own_stale)


def place_kernel(back_ref, mixed_hbm, sems, *, patch_count, uly_count):
    peers, _, width = back_ref.shape
    copies = []
    for peer in range(peers):
        columns = pl.ds(home_column(peer, patch_count, uly_count, width), width)
        copies.append(pltpu.make_async_copy(back_ref.at[peer], mixed_hbm.at[:, columns], sems.at[peer]))
        copies[-1].start()
    for copy in copies:
        copy.wait()


def place(back, patch_count, uly_count):
    peers, rows, width = back.shape
    return pl.pallas_call(
        functools.partial(place_kernel, patch_count=patch_count, uly_count=uly_count),
        out_shape=jax.ShapeDtypeStruct((rows, peers * width), jnp.bfloat16),
        in_specs=[pl.BlockSpec(memory_space=pltpu.VMEM)],
        out_specs=pl.BlockSpec(memory_space=pltpu.HBM),
        scratch_shapes=[pltpu.SemaphoreType.DMA((peers,))],
        compiler_params=pltpu.CompilerParams(vmem_limit_bytes=KERNEL_VMEM),
    )(back)


def attend_split_heads(queries, stale_kv, codes, exps):
    patch_count = lax.axis_size("patch")
    uly_count = lax.axis_size("uly")
    tokens = stale_kv.shape[0]
    width = queries.shape[1] // (patch_count * uly_count)
    both = ("patch", "uly")
    packed = pack(queries, codes, exps, patch_count, uly_count)
    own_stale = lax.dynamic_slice(stale_kv, (0, 0, lax.axis_index("patch") * width), (tokens, 2, width))
    packed, own_stale = lax.optimization_barrier((packed, jnp.swapaxes(own_stale, 0, 1)))
    blocks = lax.all_to_all(packed, both, split_axis=0, concat_axis=0, tiled=True)
    mixed = attend(blocks, own_stale)
    back = lax.all_to_all(mixed, both, split_axis=0, concat_axis=0, tiled=True)
    return place(back, patch_count, uly_count)


def on_device(queries, stale_kv, codes, exps):
    own_heads = stale_kv.shape[2] // HEAD_DIM
    if own_heads % lax.axis_size("patch") == 0:
        return attend_split_heads(queries, stale_kv, codes, exps)
    return attend_gathered(queries, stale_kv, codes, exps)


def solution(mesh):
    return jax.shard_map(
        on_device,
        mesh=mesh,
        in_specs=(
            P(("rep", "patch", "uly"), None),
            P("rep", None, "uly"),
            P(("rep", "patch", "uly"), None, None),
            P(("rep", "patch", "uly"), None, None),
        ),
        out_specs=P(("rep", "patch", "uly"), None),
        check_vma=False,
    )
```

```python
import functools
import math

import jax
import jax.numpy as jnp
from jax import lax
from jax.experimental import pallas as pl
from jax.experimental.pallas import tpu as pltpu
from jax.sharding import PartitionSpec as P

HEAD_DIM = 128
SCALE_BLOCK = 128
KERNEL_VMEM = 8 << 20
BOTH = ("patch", "uly")


def decode(codes, exps):
    num_rows = codes.shape[0]
    num_blocks = exps.shape[2]
    scaled = (
        codes.astype(jnp.float32).reshape(num_rows, 2, num_blocks, SCALE_BLOCK)
        * jnp.exp2(exps.astype(jnp.float32))[..., None]
    )
    return scaled.reshape(num_rows, 2, num_blocks * SCALE_BLOCK).astype(jnp.bfloat16)


def refresh(stale_part, resid_part):
    return (stale_part.astype(jnp.float32) + resid_part.astype(jnp.float32)).astype(jnp.bfloat16)


def column_block(rows, head):
    return rows[:, head * HEAD_DIM : (head + 1) * HEAD_DIM]


def head_scores(query_rows, key_rows, head):
    scores = lax.dot_general(
        column_block(query_rows, head),
        column_block(key_rows, head),
        (((1,), (1,)), ((), ())),
        preferred_element_type=jnp.float32,
    )
    return scores * (1.0 / math.sqrt(HEAD_DIM))


def weigh_values(weights, value_rows, head):
    return jnp.dot(
        weights.astype(jnp.bfloat16),
        column_block(value_rows, head),
        preferred_element_type=jnp.float32,
    )


def attend_whole(query_rows, kv_rows):
    head_count = query_rows.shape[1] // HEAD_DIM
    key_rows = kv_rows[:, 0]
    value_rows = kv_rows[:, 1]
    outputs = []
    for head in range(head_count):
        scores = head_scores(query_rows, key_rows, head)
        row_max = jnp.max(scores, axis=1, keepdims=True)
        weights = jnp.exp(scores - row_max)
        totals = jnp.sum(weights, axis=1, keepdims=True)
        outputs.append(weigh_values(weights, value_rows, head) / totals)
    return jnp.concatenate(outputs, axis=1).astype(jnp.bfloat16)


def attend_gathered(queries, stale_kv, codes, exps):
    residual = decode(codes, exps)
    query_rows = lax.all_to_all(queries, "uly", split_axis=1, concat_axis=0, tiled=True)
    gathered = lax.all_gather(residual, "patch", axis=0, tiled=True)
    patch_count = lax.axis_size("patch")
    blocked = gathered.reshape(patch_count, residual.shape[0], 2, residual.shape[2])
    spread = lax.all_to_all(blocked, "uly", split_axis=3, concat_axis=1, tiled=True)
    all_resid = spread.reshape(stale_kv.shape)
    result = attend_whole(query_rows, refresh(stale_kv, all_resid))
    return lax.all_to_all(result, "uly", split_axis=0, concat_axis=1, tiled=True)


def aligned(start, size):
    return pl.ds(pl.multiple_of(start, HEAD_DIM), size)


def kernel_call(body, outputs, operands, spaces, scratch=(), out_space=pltpu.VMEM):
    operands = [
        pltpu.with_memory_space_constraint(each, pltpu.HBM) if space is pltpu.HBM else each
        for each, space in zip(operands, spaces)
    ]
    return pl.pallas_call(
        body,
        out_shape=[jax.ShapeDtypeStruct(shape, jnp.bfloat16) for shape in outputs],
        in_specs=[pl.BlockSpec(memory_space=space) for space in spaces],
        out_specs=[pl.BlockSpec(memory_space=out_space)] * len(outputs),
        scratch_shapes=list(scratch),
        compiler_params=pltpu.CompilerParams(vmem_limit_bytes=KERNEL_VMEM),
    )(*operands)


def decode_kernel(queries_hbm, codes_hbm, exps_hbm, away_ref, home_ref, codes_ref, exps_ref, sems):
    _, packed_rows, width = home_ref.shape
    rows = packed_rows // 3
    uly = lax.axis_index("uly")
    letter = lax.rem(lax.axis_index("patch"), 2)
    fetch_exps = pltpu.make_async_copy(exps_hbm, exps_ref, sems.at[0])
    fetch_exps.start()
    starts = []
    fetch_codes = []
    for side in range(2):
        for turn in range(2):
            start = (((1 - uly) if side == 0 else uly) * 2 + (letter ^ turn)) * width
            starts.append(start)
            for kind in range(2):
                slot = len(fetch_codes)
                fetch_codes.append(
                    pltpu.make_async_copy(
                        codes_hbm.at[:, kind, aligned(start, width)], codes_ref.at[slot], sems.at[1 + slot]
                    )
                )
                fetch_codes[slot].start()
    fetch_queries = []
    for part, start in enumerate(starts):
        out_ref = (away_ref, home_ref)[part // 2]
        fetch_queries.append(
            pltpu.make_async_copy(
                queries_hbm.at[:, aligned(start, width)], out_ref.at[part % 2, pl.ds(2 * rows, rows)], sems.at[9 + part]
            )
        )
        fetch_queries[-1].start()
    blocks = exps_ref.shape[2]
    block_of = lax.broadcasted_iota(jnp.int32, (blocks, width), 1) // SCALE_BLOCK
    row_of = lax.broadcasted_iota(jnp.int32, (blocks, width), 0)
    fetch_exps.wait()
    scales = [jnp.exp2(exps_ref[:, kind, :].astype(jnp.float32)).astype(jnp.bfloat16) for kind in range(2)]
    for part, start in enumerate(starts):
        out_ref = (away_ref, home_ref)[part // 2]
        spread = (row_of == block_of + start // SCALE_BLOCK).astype(jnp.float32).astype(jnp.bfloat16)
        for kind in range(2):
            scale = jnp.dot(scales[kind], spread, preferred_element_type=jnp.float32)
            fetch_codes[2 * part + kind].wait()
            decoded = codes_ref[2 * part + kind].astype(jnp.float32) * scale
            out_ref[part % 2, kind * rows : (kind + 1) * rows, :] = decoded.astype(jnp.bfloat16)
    for fetch in fetch_queries:
        fetch.wait()


def decode_halves(queries, codes, exps):
    rows, model_width = queries.shape
    quarter = model_width // lax.axis_size("uly") // 2
    return kernel_call(
        decode_kernel,
        [(2, 3 * rows, quarter)] * 2,
        [queries, codes, exps],
        [pltpu.HBM] * 3,
        [
            pltpu.VMEM((8, rows, quarter), codes.dtype),
            pltpu.VMEM(exps.shape, exps.dtype),
            pltpu.SemaphoreType.DMA((13,)),
        ],
    )


def attend_kernel(home_ref, received_ref, near_ref, far_refs, cross_refs, stale_ref, *out_refs):
    rows, width = out_refs[0].shape
    patch = lax.axis_index("patch")
    uly = lax.axis_index("uly")
    heads = range(width // HEAD_DIM)
    sources = (
        (home_ref.at[0], received_ref.at[0]),
        (near_ref.at[0], near_ref.at[1]),
        far_refs,
        cross_refs,
    )

    def refreshed(kind):
        parts = []
        for step, pair in enumerate(sources):
            for side, source_ref in enumerate(pair):
                block = (patch ^ step) * 2 + (uly ^ side)
                stale = stale_ref[kind, pl.ds(pl.multiple_of(block * rows, rows), rows), :]
                parts.append(refresh(stale, source_ref[kind * rows : (kind + 1) * rows, :]))
        return jnp.concatenate(parts, axis=0)

    query_rows = jnp.concatenate(
        [source_ref[2 * rows : 3 * rows, :] for pair in sources[:2] for source_ref in pair], axis=0
    )
    key_rows = refreshed(0)
    scores = [head_scores(query_rows, key_rows, head) for head in heads]
    value_rows = refreshed(1)
    weights = [jnp.exp(each - jnp.max(each, axis=1, keepdims=True)) for each in scores]
    sums = [weigh_values(weights[head], value_rows, head) for head in heads]
    for head in heads:
        result = (sums[head] / jnp.sum(weights[head], axis=1, keepdims=True)).astype(jnp.bfloat16)
        for block, out_ref in enumerate(out_refs):
            out_ref[:, head * HEAD_DIM : (head + 1) * HEAD_DIM] = result[block * rows : (block + 1) * rows]


def attend_quarter(home, received, near, far, cross, own_stale):
    rows, width = home.shape[1] // 3, home.shape[2]

    def body(home_ref, received_ref, near_ref, far_a, far_b, cross_a, cross_b, stale_ref, *out_refs):
        attend_kernel(home_ref, received_ref, near_ref, (far_a, far_b), (cross_a, cross_b), stale_ref, *out_refs)

    return kernel_call(body, [(rows, width)] * 4, [home, received, near, *far, *cross, own_stale], [pltpu.VMEM] * 8)


def place_kernel(*refs):
    *part_refs, mixed_hbm, sems = refs
    width = part_refs[0].shape[1]
    uly = lax.axis_index("uly")
    letter = lax.rem(lax.axis_index("patch"), 2)
    copies = []
    for block, part_ref in enumerate(part_refs):
        start = ((uly ^ (block & 1)) * 2 + (letter ^ (block >> 1))) * width
        copies.append(pltpu.make_async_copy(part_ref, mixed_hbm.at[:, aligned(start, width)], sems.at[block]))
        copies[-1].start()
    for copy in copies:
        copy.wait()


def place(parts):
    rows, width = parts[0].shape
    (mixed,) = kernel_call(
        place_kernel,
        [(rows, 4 * width)],
        parts,
        [pltpu.VMEM] * 4,
        [pltpu.SemaphoreType.DMA((4,))],
        out_space=pltpu.HBM,
    )
    return mixed


def swap(array, distance):
    count = lax.axis_size(BOTH)
    return lax.ppermute(array, BOTH, [(peer, peer ^ distance) for peer in range(count)])


def attend_paired(queries, stale_kv, codes, exps):
    tokens = stale_kv.shape[0]
    quarter = stale_kv.shape[2] // 2
    kv_rows = 2 * queries.shape[0]
    away, home = decode_halves(queries, codes, exps)
    received = swap(away, 1)
    home, stale_kv = lax.optimization_barrier((home, stale_kv))
    letter = lax.rem(lax.axis_index("patch"), 2)
    own_stale = jnp.swapaxes(lax.dynamic_slice(stale_kv, (0, 0, letter * quarter), (tokens, 2, quarter)), 0, 1)
    cross = [swap(each[1, :kv_rows], 6) for each in (home, received)]
    far = [swap(each[0, :kv_rows], 4) for each in (home, received)]
    near = swap(jnp.stack([home[1], received[1]]), 2)
    parts = attend_quarter(home, received, near, far, cross, own_stale)
    return place([parts[0]] + [swap(parts[block], block) for block in (1, 2, 3)])


def on_device(queries, stale_kv, codes, exps):
    if lax.axis_size("patch") == 4 and lax.axis_size("uly") == 2:
        return attend_paired(queries, stale_kv, codes, exps)
    return attend_gathered(queries, stale_kv, codes, exps)


def solution(mesh):
    return jax.shard_map(
        on_device,
        mesh=mesh,
        in_specs=(
            P(("rep", "patch", "uly"), None),
            P("rep", None, "uly"),
            P(("rep", "patch", "uly"), None, None),
            P(("rep", "patch", "uly"), None, None),
        ),
        out_specs=P(("rep", "patch", "uly"), None),
        check_vma=False,
    )
```

```python
import functools
import math

import jax
import jax.numpy as jnp
from jax import lax
from jax.experimental import pallas as pl
from jax.experimental.pallas import tpu as pltpu
from jax.sharding import PartitionSpec as P

HEAD_DIM = 128
SCALE_BLOCK = 128
KERNEL_VMEM = 8 << 20
BOTH = ("patch", "uly")
RETURN_ORDER = (3, 1, 2)


def decode(codes, exps):
    num_rows = codes.shape[0]
    num_blocks = exps.shape[2]
    scaled = (
        codes.astype(jnp.float32).reshape(num_rows, 2, num_blocks, SCALE_BLOCK)
        * jnp.exp2(exps.astype(jnp.float32))[..., None]
    )
    return scaled.reshape(num_rows, 2, num_blocks * SCALE_BLOCK).astype(jnp.bfloat16)


def refresh(stale_part, resid_part):
    return (stale_part.astype(jnp.float32) + resid_part.astype(jnp.float32)).astype(jnp.bfloat16)


def column_block(rows, head):
    return rows[:, head * HEAD_DIM : (head + 1) * HEAD_DIM]


def head_scores(query_rows, key_rows, head):
    scores = lax.dot_general(
        column_block(query_rows, head),
        column_block(key_rows, head),
        (((1,), (1,)), ((), ())),
        preferred_element_type=jnp.float32,
    )
    return scores * (1.0 / math.sqrt(HEAD_DIM))


def weigh_values(weights, value_rows, head):
    return jnp.dot(
        weights.astype(jnp.bfloat16),
        column_block(value_rows, head),
        preferred_element_type=jnp.float32,
    )


def attend_whole(query_rows, kv_rows):
    head_count = query_rows.shape[1] // HEAD_DIM
    key_rows = kv_rows[:, 0]
    value_rows = kv_rows[:, 1]
    outputs = []
    for head in range(head_count):
        scores = head_scores(query_rows, key_rows, head)
        row_max = jnp.max(scores, axis=1, keepdims=True)
        weights = jnp.exp(scores - row_max)
        totals = jnp.sum(weights, axis=1, keepdims=True)
        outputs.append(weigh_values(weights, value_rows, head) / totals)
    return jnp.concatenate(outputs, axis=1).astype(jnp.bfloat16)


def attend_gathered(queries, stale_kv, codes, exps):
    residual = decode(codes, exps)
    query_rows = lax.all_to_all(queries, "uly", split_axis=1, concat_axis=0, tiled=True)
    gathered = lax.all_gather(residual, "patch", axis=0, tiled=True)
    patch_count = lax.axis_size("patch")
    blocked = gathered.reshape(patch_count, residual.shape[0], 2, residual.shape[2])
    spread = lax.all_to_all(blocked, "uly", split_axis=3, concat_axis=1, tiled=True)
    all_resid = spread.reshape(stale_kv.shape)
    result = attend_whole(query_rows, refresh(stale_kv, all_resid))
    return lax.all_to_all(result, "uly", split_axis=0, concat_axis=1, tiled=True)


def aligned(start, size):
    return pl.ds(pl.multiple_of(start, HEAD_DIM), size)


def kernel_call(body, outputs, operands, spaces, scratch=(), out_space=pltpu.VMEM):
    operands = [
        pltpu.with_memory_space_constraint(each, pltpu.HBM) if space is pltpu.HBM else each
        for each, space in zip(operands, spaces)
    ]
    return pl.pallas_call(
        body,
        out_shape=[jax.ShapeDtypeStruct(shape, jnp.bfloat16) for shape in outputs],
        in_specs=[pl.BlockSpec(memory_space=space) for space in spaces],
        out_specs=[pl.BlockSpec(memory_space=out_space)] * len(outputs),
        scratch_shapes=list(scratch),
        compiler_params=pltpu.CompilerParams(vmem_limit_bytes=KERNEL_VMEM),
    )(*operands)


def decode_kernel(queries_hbm, codes_hbm, exps_hbm, away_ref, home_ref, codes_ref, exps_ref, sems):
    _, packed_rows, width = home_ref.shape
    rows = packed_rows // 3
    uly = lax.axis_index("uly")
    letter = lax.rem(lax.axis_index("patch"), 2)
    fetch_exps = pltpu.make_async_copy(exps_hbm, exps_ref, sems.at[0])
    fetch_exps.start()
    starts = []
    fetch_codes = []
    for side in range(2):
        for turn in range(2):
            start = (((1 - uly) if side == 0 else uly) * 2 + (letter ^ turn)) * width
            starts.append(start)
            for kind in range(2):
                slot = len(fetch_codes)
                fetch_codes.append(
                    pltpu.make_async_copy(
                        codes_hbm.at[:, kind, aligned(start, width)], codes_ref.at[slot], sems.at[1 + slot]
                    )
                )
                fetch_codes[slot].start()
    fetch_queries = []
    for part, start in enumerate(starts):
        out_ref = (away_ref, home_ref)[part // 2]
        fetch_queries.append(
            pltpu.make_async_copy(
                queries_hbm.at[:, aligned(start, width)], out_ref.at[part % 2, pl.ds(2 * rows, rows)], sems.at[9 + part]
            )
        )
        fetch_queries[-1].start()
    blocks = exps_ref.shape[2]
    block_of = lax.broadcasted_iota(jnp.int32, (blocks, width), 1) // SCALE_BLOCK
    row_of = lax.broadcasted_iota(jnp.int32, (blocks, width), 0)
    fetch_exps.wait()
    scales = jnp.concatenate([jnp.exp2(exps_ref[:, kind, :].astype(jnp.float32)) for kind in range(2)], axis=0)
    scales = scales.astype(jnp.bfloat16)
    spreads = [(row_of == block_of + start // SCALE_BLOCK).astype(jnp.float32).astype(jnp.bfloat16) for start in starts]
    wide_scales = [jnp.dot(scales, spread, preferred_element_type=jnp.float32) for spread in spreads]
    for part, wide_scale in enumerate(wide_scales):
        out_ref = (away_ref, home_ref)[part // 2]
        for kind in range(2):
            fetch_codes[2 * part + kind].wait()
            own_rows = slice(kind * rows, (kind + 1) * rows)
            decoded = codes_ref[2 * part + kind].astype(jnp.float32) * wide_scale[own_rows]
            out_ref[part % 2, own_rows, :] = decoded.astype(jnp.bfloat16)
    for fetch in fetch_queries:
        fetch.wait()


def decode_halves(queries, codes, exps):
    rows, model_width = queries.shape
    quarter = model_width // lax.axis_size("uly") // 2
    return kernel_call(
        decode_kernel,
        [(2, 3 * rows, quarter)] * 2,
        [queries, codes, exps],
        [pltpu.HBM] * 3,
        [
            pltpu.VMEM((8, rows, quarter), codes.dtype),
            pltpu.VMEM(exps.shape, exps.dtype),
            pltpu.SemaphoreType.DMA((13,)),
        ],
    )


def attend_kernel(home_ref, received_ref, near_ref, far_refs, cross_refs, stale_ref, *out_refs):
    rows, width = out_refs[0].shape
    patch = lax.axis_index("patch")
    uly = lax.axis_index("uly")
    heads = range(width // HEAD_DIM)
    sources = (
        (home_ref.at[0], received_ref.at[0]),
        (near_ref.at[0], near_ref.at[1]),
        far_refs,
        cross_refs,
    )

    def refreshed(kind):
        parts = []
        for step, pair in enumerate(sources):
            for side, source_ref in enumerate(pair):
                block = (patch ^ step) * 2 + (uly ^ side)
                stale = stale_ref[kind, pl.ds(pl.multiple_of(block * rows, rows), rows), :]
                parts.append(refresh(stale, source_ref[kind * rows : (kind + 1) * rows, :]))
        return jnp.concatenate(parts, axis=0)

    query_rows = jnp.concatenate(
        [source_ref[2 * rows : 3 * rows, :] for pair in sources[:2] for source_ref in pair], axis=0
    )
    key_rows = refreshed(0)
    scores = [head_scores(query_rows, key_rows, head) for head in heads]
    value_rows = refreshed(1)
    weights = [jnp.exp(each - jnp.max(each, axis=1, keepdims=True)) for each in scores]
    sums = [weigh_values(weights[head], value_rows, head) for head in heads]
    for head in heads:
        result = (sums[head] / jnp.sum(weights[head], axis=1, keepdims=True)).astype(jnp.bfloat16)
        for block, out_ref in enumerate(out_refs):
            out_ref[:, head * HEAD_DIM : (head + 1) * HEAD_DIM] = result[block * rows : (block + 1) * rows]


def attend_quarter(home, received, near, far, cross, own_stale):
    rows, width = home.shape[1] // 3, home.shape[2]

    def body(home_ref, received_ref, cross_a, far_a, cross_b, far_b, near_ref, stale_ref, *out_refs):
        attend_kernel(home_ref, received_ref, near_ref, (far_a, far_b), (cross_a, cross_b), stale_ref, *out_refs)

    return kernel_call(body, [(rows, width)] * 4, [home, received, cross[0], far[0], cross[1], far[1], near, own_stale], [pltpu.VMEM] * 8)


def place_kernel(*refs):
    *part_refs, mixed_hbm, sems = refs
    width = part_refs[0].shape[1]
    uly = lax.axis_index("uly")
    letter = lax.rem(lax.axis_index("patch"), 2)
    copies = []
    for block, part_ref in zip((0, *RETURN_ORDER), part_refs):
        start = ((uly ^ (block & 1)) * 2 + (letter ^ (block >> 1))) * width
        copies.append(pltpu.make_async_copy(part_ref, mixed_hbm.at[:, aligned(start, width)], sems.at[block]))
        copies[-1].start()
    for copy in copies:
        copy.wait()


def place(parts):
    rows, width = parts[0].shape
    (mixed,) = kernel_call(
        place_kernel,
        [(rows, 4 * width)],
        parts,
        [pltpu.VMEM] * 4,
        [pltpu.SemaphoreType.DMA((4,))],
        out_space=pltpu.HBM,
    )
    return mixed


def swap(array, distance):
    count = lax.axis_size(BOTH)
    return lax.ppermute(array, BOTH, [(peer, peer ^ distance) for peer in range(count)])


def attend_paired(queries, stale_kv, codes, exps):
    tokens = stale_kv.shape[0]
    quarter = stale_kv.shape[2] // 2
    kv_rows = 2 * queries.shape[0]
    away, home = decode_halves(queries, codes, exps)
    received = swap(away, 1)
    home, stale_kv = lax.optimization_barrier((home, stale_kv))
    letter = lax.rem(lax.axis_index("patch"), 2)
    own_stale = jnp.swapaxes(lax.dynamic_slice(stale_kv, (0, 0, letter * quarter), (tokens, 2, quarter)), 0, 1)
    cross = [swap(each[1, :kv_rows], 6) for each in (home, received)]
    far = [swap(each[0, :kv_rows], 4) for each in (home, received)]
    near = swap(jnp.stack([home[1], received[1]]), 2)
    parts = attend_quarter(home, received, near, far, cross, own_stale)
    return place([parts[0]] + [swap(parts[block], block) for block in RETURN_ORDER])


def on_device(queries, stale_kv, codes, exps):
    if lax.axis_size("patch") == 4 and lax.axis_size("uly") == 2:
        return attend_paired(queries, stale_kv, codes, exps)
    return attend_gathered(queries, stale_kv, codes, exps)


def solution(mesh):
    return jax.shard_map(
        on_device,
        mesh=mesh,
        in_specs=(
            P(("rep", "patch", "uly"), None),
            P("rep", None, "uly"),
            P(("rep", "patch", "uly"), None, None),
            P(("rep", "patch", "uly"), None, None),
        ),
        out_specs=P(("rep", "patch", "uly"), None),
        check_vma=False,
    )
```

```python
import functools
import math

import jax
import jax.numpy as jnp
from jax import lax
from jax.experimental import pallas as pl
from jax.experimental.pallas import tpu as pltpu
from jax.sharding import PartitionSpec as P

HEAD_DIM = 128
SCALE_BLOCK = 128
KERNEL_VMEM = 8 << 20
BOTH = ("patch", "uly")
START_ORDER = (5, 4, 1, 3, 2)
RETURN_ORDER = (3, 1, 2)
SPLIT_TERMS = 3


def decode(codes, exps):
    num_rows = codes.shape[0]
    num_blocks = exps.shape[2]
    scaled = (
        codes.astype(jnp.float32).reshape(num_rows, 2, num_blocks, SCALE_BLOCK)
        * jnp.exp2(exps.astype(jnp.float32))[..., None]
    )
    return scaled.reshape(num_rows, 2, num_blocks * SCALE_BLOCK).astype(jnp.bfloat16)


def refresh(stale_part, resid_part):
    return (stale_part.astype(jnp.float32) + resid_part.astype(jnp.float32)).astype(jnp.bfloat16)


def column_block(rows, head):
    return rows[:, head * HEAD_DIM : (head + 1) * HEAD_DIM]


def head_scores(query_rows, key_rows, head):
    scores = lax.dot_general(
        column_block(query_rows, head),
        column_block(key_rows, head),
        (((1,), (1,)), ((), ())),
        preferred_element_type=jnp.float32,
    )
    return scores * (1.0 / math.sqrt(HEAD_DIM))


def weigh_values(weights, value_rows, head):
    return jnp.dot(
        weights.astype(jnp.bfloat16),
        column_block(value_rows, head),
        preferred_element_type=jnp.float32,
    )


def attend_whole(query_rows, kv_rows):
    head_count = query_rows.shape[1] // HEAD_DIM
    key_rows = kv_rows[:, 0]
    value_rows = kv_rows[:, 1]
    outputs = []
    for head in range(head_count):
        scores = head_scores(query_rows, key_rows, head)
        row_max = jnp.max(scores, axis=1, keepdims=True)
        weights = jnp.exp(scores - row_max)
        totals = jnp.sum(weights, axis=1, keepdims=True)
        outputs.append(weigh_values(weights, value_rows, head) / totals)
    return jnp.concatenate(outputs, axis=1).astype(jnp.bfloat16)


def attend_gathered(queries, stale_kv, codes, exps):
    residual = decode(codes, exps)
    query_rows = lax.all_to_all(queries, "uly", split_axis=1, concat_axis=0, tiled=True)
    gathered = lax.all_gather(residual, "patch", axis=0, tiled=True)
    patch_count = lax.axis_size("patch")
    blocked = gathered.reshape(patch_count, residual.shape[0], 2, residual.shape[2])
    spread = lax.all_to_all(blocked, "uly", split_axis=3, concat_axis=1, tiled=True)
    all_resid = spread.reshape(stale_kv.shape)
    result = attend_whole(query_rows, refresh(stale_kv, all_resid))
    return lax.all_to_all(result, "uly", split_axis=0, concat_axis=1, tiled=True)


def aligned(start, size):
    return pl.ds(pl.multiple_of(start, HEAD_DIM), size)


def kernel_call(body, outputs, operands, spaces, scratch=(), out_space=pltpu.VMEM):
    operands = [
        pltpu.with_memory_space_constraint(each, pltpu.HBM) if space is pltpu.HBM else each
        for each, space in zip(operands, spaces)
    ]
    return pl.pallas_call(
        body,
        out_shape=[jax.ShapeDtypeStruct(shape, jnp.bfloat16) for shape in outputs],
        in_specs=[pl.BlockSpec(memory_space=space) for space in spaces],
        out_specs=[pl.BlockSpec(memory_space=out_space)] * len(outputs),
        scratch_shapes=list(scratch),
        compiler_params=pltpu.CompilerParams(vmem_limit_bytes=KERNEL_VMEM),
    )(*operands)


def decode_kernel(queries_hbm, codes_hbm, exps_hbm, away_ref, home_ref, home_queries_ref, codes_ref, exps_ref, sems):
    rows, half = home_queries_ref.shape
    uly = lax.axis_index("uly")
    starts = ((1 - uly) * half, uly * half)
    fetch_exps = pltpu.make_async_copy(exps_hbm, exps_ref, sems.at[0])
    fetch_exps.start()
    fetch_codes = []
    for start in starts:
        for kind in range(2):
            slot = len(fetch_codes)
            fetch_codes.append(
                pltpu.make_async_copy(codes_hbm.at[:, kind, aligned(start, half)], codes_ref.at[slot], sems.at[1 + slot])
            )
            fetch_codes[slot].start()
    fetch_queries = []
    for side, target in enumerate((away_ref.at[pl.ds(2 * rows, rows)], home_queries_ref)):
        fetch_queries.append(pltpu.make_async_copy(queries_hbm.at[:, aligned(starts[side], half)], target, sems.at[5 + side]))
        fetch_queries[side].start()
    blocks = exps_ref.shape[2]
    block_of = lax.broadcasted_iota(jnp.int32, (blocks, half), 1) // SCALE_BLOCK
    row_of = lax.broadcasted_iota(jnp.int32, (blocks, half), 0)
    fetch_exps.wait()
    scales = jnp.concatenate([jnp.exp2(exps_ref[:, kind, :].astype(jnp.float32)) for kind in range(2)], axis=0)
    scales = scales.astype(jnp.bfloat16)
    spreads = [(row_of == block_of + start // SCALE_BLOCK).astype(jnp.float32).astype(jnp.bfloat16) for start in starts]
    wide_scales = [jnp.dot(scales, spread, preferred_element_type=jnp.float32) for spread in spreads]
    for side, out_ref in enumerate((away_ref, home_ref)):
        for kind in range(2):
            fetch_codes[2 * side + kind].wait()
            own_rows = slice(kind * rows, (kind + 1) * rows)
            decoded = codes_ref[2 * side + kind].astype(jnp.float32) * wide_scales[side][own_rows]
            out_ref[own_rows, :] = decoded.astype(jnp.bfloat16)
    for fetch in fetch_queries:
        fetch.wait()


def decode_halves(queries, codes, exps):
    rows, model_width = queries.shape
    half = model_width // lax.axis_size("uly")
    return kernel_call(
        decode_kernel,
        [(3 * rows, half), (2 * rows, half), (rows, half)],
        [queries, codes, exps],
        [pltpu.HBM] * 3,
        [
            pltpu.VMEM((4, rows, half), codes.dtype),
            pltpu.VMEM(exps.shape, exps.dtype),
            pltpu.SemaphoreType.DMA((7,)),
        ],
    )


def lane_groups(heads):
    lane = lax.broadcasted_iota(jnp.int32, (1, HEAD_DIM), 1)
    return [(lane >= group * heads) & (lane < (group + 1) * heads) for group in range(2 * SPLIT_TERMS)], lane


def pack_stats(maxima, totals):
    heads = len(maxima)
    groups, lane = lane_groups(heads)
    is_maximum = lane < SPLIT_TERMS * heads
    left = jnp.zeros((maxima[0].shape[0], HEAD_DIM), jnp.float32)
    for head in range(heads):
        here = lane == head
        for group in range(1, 2 * SPLIT_TERMS):
            here = here | (lane == head + group * heads)
        left = jnp.where(here, jnp.where(is_maximum, maxima[head], totals[head]), left)
    packed = jnp.zeros_like(left)
    for term in range(SPLIT_TERMS):
        rounded = left.astype(jnp.bfloat16).astype(jnp.float32)
        packed = jnp.where(groups[term] | groups[SPLIT_TERMS + term], rounded, packed)
        left = left - rounded
    return packed.astype(jnp.bfloat16)


def unpack_stats(packed, heads):
    terms = packed.astype(jnp.float32)
    summed = terms
    for term in range(1, SPLIT_TERMS):
        summed = summed + pltpu.roll(terms, HEAD_DIM - term * heads, 1)
    return summed, pltpu.roll(summed, HEAD_DIM - SPLIT_TERMS * heads, 1)


def attend_kernel(stale_ref, query_parts, key_value_parts, out_refs):
    rows = query_parts[0].shape[0]
    width = query_parts[0].shape[1]
    patch = lax.axis_index("patch")
    uly = lax.axis_index("uly")
    heads = range(width // HEAD_DIM)

    def refreshed(kind):
        parts = []
        for block, part_ref in enumerate(key_value_parts):
            home = (patch ^ (block & 2)) * 2 + (uly ^ (block & 1))
            stale = stale_ref[kind, pl.ds(pl.multiple_of(home * rows, rows), rows), :]
            parts.append(refresh(stale, part_ref[kind * rows : (kind + 1) * rows, :]))
        return jnp.concatenate(parts, axis=0)

    query_rows = jnp.concatenate([part_ref[...] for part_ref in query_parts], axis=0)
    key_rows = refreshed(0)
    scores = [head_scores(query_rows, key_rows, head) for head in heads]
    value_rows = refreshed(1)
    maxima = [jnp.max(each, axis=1, keepdims=True) for each in scores]
    weights = [jnp.exp(each - maximum) for each, maximum in zip(scores, maxima)]
    sums = [weigh_values(weights[head], value_rows, head) for head in heads]
    totals = [jnp.sum(each, axis=1, keepdims=True) for each in weights]
    for head in heads:
        result = (sums[head] / totals[head]).astype(jnp.bfloat16)
        for block, out_ref in enumerate(out_refs):
            out_ref[:, head * HEAD_DIM : (head + 1) * HEAD_DIM] = result[block * rows : (block + 1) * rows]
    stats = pack_stats(maxima, totals)
    for block, out_ref in enumerate(out_refs):
        out_ref[:, width : width + HEAD_DIM] = stats[block * rows : (block + 1) * rows]


def attend_partly(home, home_queries, arrived, own_stale):
    rows, width = home_queries.shape

    def body(home_ref, home_queries_ref, *refs):
        named = dict(zip(START_ORDER, refs))
        stale_ref, *out_refs = refs[len(START_ORDER) :]
        query_parts = (home_queries_ref, named[1].at[pl.ds(2 * rows, rows)], named[2], named[3])
        attend_kernel(stale_ref, query_parts, (home_ref, named[1], named[4], named[5]), out_refs)

    operands = [home, home_queries, *(arrived[name] for name in START_ORDER), own_stale]
    return kernel_call(body, [(rows, width + HEAD_DIM)] * 4, operands, [pltpu.VMEM] * len(operands))


def merge_kernel(part_refs, mixed_hbm, mixed_ref, sems):
    rows, packed_width = part_refs[0].shape
    width = packed_width - HEAD_DIM
    heads = width // HEAD_DIM
    uly = lax.axis_index("uly")
    stats = [unpack_stats(part_ref[:, width:], heads) for part_ref in part_refs]
    used = lax.broadcasted_iota(jnp.int32, (1, HEAD_DIM), 1) < heads
    shares = []
    for near, far in ((0, 2), (1, 3)):
        top = jnp.maximum(stats[near][0], stats[far][0])
        near_total = stats[near][1] * jnp.exp(stats[near][0] - top)
        far_total = stats[far][1] * jnp.exp(stats[far][0] - top)
        share = jnp.where(used, near_total / (near_total + far_total), 0.0)
        high = share.astype(jnp.bfloat16)
        shares += [high, (share - high.astype(jnp.float32)).astype(jnp.bfloat16)]
    head_of = lax.broadcasted_iota(jnp.int32, (HEAD_DIM, width), 1) // HEAD_DIM
    spread = (lax.broadcasted_iota(jnp.int32, (HEAD_DIM, width), 0) == head_of).astype(jnp.float32).astype(jnp.bfloat16)
    wide = jnp.dot(jnp.concatenate(shares, axis=0), spread, preferred_element_type=jnp.float32)
    copies = []
    for side, (near, far) in enumerate(((0, 2), (1, 3))):
        share = wide[2 * side * rows : (2 * side + 1) * rows] + wide[(2 * side + 1) * rows : (2 * side + 2) * rows]
        far_rows = part_refs[far][:, :width].astype(jnp.float32)
        near_rows = part_refs[near][:, :width].astype(jnp.float32)
        mixed_ref[side] = (far_rows + (near_rows - far_rows) * share).astype(jnp.bfloat16)
        columns = aligned((uly if side == 0 else 1 - uly) * width, width)
        copies.append(pltpu.make_async_copy(mixed_ref.at[side], mixed_hbm.at[:, columns], sems.at[side]))
        copies[side].start()
    for copy in copies:
        copy.wait()


def merge(parts):
    rows, packed_width = parts[0].shape
    width = packed_width - HEAD_DIM
    names = (0, *RETURN_ORDER)

    def body(*refs):
        named = dict(zip(names, refs))
        merge_kernel([named[block] for block in range(4)], *refs[4:])

    (mixed,) = kernel_call(
        body,
        [(rows, 2 * width)],
        [parts[name] for name in names],
        [pltpu.VMEM] * 4,
        [pltpu.VMEM((2, rows, width), jnp.bfloat16), pltpu.SemaphoreType.DMA((2,))],
        out_space=pltpu.HBM,
    )
    return mixed


def swap(array, distance):
    count = lax.axis_size(BOTH)
    return lax.ppermute(array, BOTH, [(peer, peer ^ distance) for peer in range(count)])


def attend_paired(queries, stale_kv, codes, exps):
    kv_rows = 2 * queries.shape[0]
    away, home, home_queries = decode_halves(queries, codes, exps)
    home, stale_kv = lax.optimization_barrier((home, stale_kv))
    own_stale = jnp.swapaxes(stale_kv, 0, 1)
    blocks = {1: away, 2: home_queries, 3: away[kv_rows:], 4: home, 5: away[:kv_rows]}
    arrived = {distance: swap(blocks[distance], distance) for distance in START_ORDER}
    parts = attend_partly(home, home_queries, arrived, own_stale)
    return merge([parts[0]] + [swap(parts[distance], distance) for distance in (1, 2, 3)])


def on_device(queries, stale_kv, codes, exps):
    if lax.axis_size("patch") == 4 and lax.axis_size("uly") == 2:
        return attend_paired(queries, stale_kv, codes, exps)
    return attend_gathered(queries, stale_kv, codes, exps)


def solution(mesh):
    return jax.shard_map(
        on_device,
        mesh=mesh,
        in_specs=(
            P(("rep", "patch", "uly"), None),
            P("rep", None, "uly"),
            P(("rep", "patch", "uly"), None, None),
            P(("rep", "patch", "uly"), None, None),
        ),
        out_specs=P(("rep", "patch", "uly"), None),
        check_vma=False,
    )
```

```python
import functools
import math

import jax
import jax.numpy as jnp
from jax import lax
from jax.experimental import pallas as pl
from jax.experimental.pallas import tpu as pltpu
from jax.sharding import PartitionSpec as P

HEAD_DIM = 128
SCALE_BLOCK = 128
KERNEL_VMEM = 8 << 20
BOTH = ("patch", "uly")
RETURN_ORDER = (3, 2, 1)
SPLIT_TERMS = 3


def decode(codes, exps):
    num_rows = codes.shape[0]
    num_blocks = exps.shape[2]
    scaled = (
        codes.astype(jnp.float32).reshape(num_rows, 2, num_blocks, SCALE_BLOCK)
        * jnp.exp2(exps.astype(jnp.float32))[..., None]
    )
    return scaled.reshape(num_rows, 2, num_blocks * SCALE_BLOCK).astype(jnp.bfloat16)


def refresh(stale_part, resid_part):
    return (stale_part.astype(jnp.float32) + resid_part.astype(jnp.float32)).astype(jnp.bfloat16)


def column_block(rows, head):
    return rows[:, head * HEAD_DIM : (head + 1) * HEAD_DIM]


def head_scores(query_rows, key_rows, head):
    scores = lax.dot_general(
        column_block(query_rows, head),
        column_block(key_rows, head),
        (((1,), (1,)), ((), ())),
        preferred_element_type=jnp.float32,
    )
    return scores * (1.0 / math.sqrt(HEAD_DIM))


def weigh_values(weights, value_rows, head):
    return jnp.dot(
        weights.astype(jnp.bfloat16),
        column_block(value_rows, head),
        preferred_element_type=jnp.float32,
    )


def attend_whole(query_rows, kv_rows):
    head_count = query_rows.shape[1] // HEAD_DIM
    key_rows = kv_rows[:, 0]
    value_rows = kv_rows[:, 1]
    outputs = []
    for head in range(head_count):
        scores = head_scores(query_rows, key_rows, head)
        row_max = jnp.max(scores, axis=1, keepdims=True)
        weights = jnp.exp(scores - row_max)
        totals = jnp.sum(weights, axis=1, keepdims=True)
        outputs.append(weigh_values(weights, value_rows, head) / totals)
    return jnp.concatenate(outputs, axis=1).astype(jnp.bfloat16)


def attend_gathered(queries, stale_kv, codes, exps):
    residual = decode(codes, exps)
    query_rows = lax.all_to_all(queries, "uly", split_axis=1, concat_axis=0, tiled=True)
    gathered = lax.all_gather(residual, "patch", axis=0, tiled=True)
    patch_count = lax.axis_size("patch")
    blocked = gathered.reshape(patch_count, residual.shape[0], 2, residual.shape[2])
    spread = lax.all_to_all(blocked, "uly", split_axis=3, concat_axis=1, tiled=True)
    all_resid = spread.reshape(stale_kv.shape)
    result = attend_whole(query_rows, refresh(stale_kv, all_resid))
    return lax.all_to_all(result, "uly", split_axis=0, concat_axis=1, tiled=True)


def aligned(start, size):
    return pl.ds(pl.multiple_of(start, HEAD_DIM), size)


def kernel_call(body, outputs, operands, spaces, scratch=(), out_space=pltpu.VMEM):
    operands = [
        pltpu.with_memory_space_constraint(each, pltpu.HBM) if space is pltpu.HBM else each
        for each, space in zip(operands, spaces)
    ]
    return pl.pallas_call(
        body,
        out_shape=[jax.ShapeDtypeStruct(shape, jnp.bfloat16) for shape in outputs],
        in_specs=[pl.BlockSpec(memory_space=space) for space in spaces],
        out_specs=[pl.BlockSpec(memory_space=out_space)] * len(outputs),
        scratch_shapes=list(scratch),
        compiler_params=pltpu.CompilerParams(vmem_limit_bytes=KERNEL_VMEM),
    )(*operands)


def decode_kernel(queries_hbm, codes_hbm, exps_hbm, away_ref, home_ref, home_queries_ref, codes_ref, exps_ref, sems):
    rows, half = home_queries_ref.shape
    uly = lax.axis_index("uly")
    starts = ((1 - uly) * half, uly * half)
    fetch_exps = pltpu.make_async_copy(exps_hbm, exps_ref, sems.at[0])
    fetch_exps.start()
    fetch_codes = []
    for start in starts:
        for kind in range(2):
            slot = len(fetch_codes)
            fetch_codes.append(
                pltpu.make_async_copy(codes_hbm.at[:, kind, aligned(start, half)], codes_ref.at[slot], sems.at[1 + slot])
            )
            fetch_codes[slot].start()
    fetch_queries = []
    for side, target in enumerate((away_ref.at[pl.ds(2 * rows, rows)], home_queries_ref)):
        fetch_queries.append(pltpu.make_async_copy(queries_hbm.at[:, aligned(starts[side], half)], target, sems.at[5 + side]))
        fetch_queries[side].start()
    blocks = exps_ref.shape[2]
    block_of = lax.broadcasted_iota(jnp.int32, (blocks, half), 1) // SCALE_BLOCK
    row_of = lax.broadcasted_iota(jnp.int32, (blocks, half), 0)
    fetch_exps.wait()
    scales = jnp.concatenate([jnp.exp2(exps_ref[:, kind, :].astype(jnp.float32)) for kind in range(2)], axis=0)
    scales = scales.astype(jnp.bfloat16)
    spreads = [(row_of == block_of + start // SCALE_BLOCK).astype(jnp.float32).astype(jnp.bfloat16) for start in starts]
    wide_scales = [jnp.dot(scales, spread, preferred_element_type=jnp.float32) for spread in spreads]
    for side, out_ref in enumerate((away_ref, home_ref)):
        for kind in range(2):
            fetch_codes[2 * side + kind].wait()
            own_rows = slice(kind * rows, (kind + 1) * rows)
            decoded = codes_ref[2 * side + kind].astype(jnp.float32) * wide_scales[side][own_rows]
            out_ref[own_rows, :] = decoded.astype(jnp.bfloat16)
    for fetch in fetch_queries:
        fetch.wait()


def decode_halves(queries, codes, exps):
    rows, model_width = queries.shape
    half = model_width // lax.axis_size("uly")
    return kernel_call(
        decode_kernel,
        [(3 * rows, half), (2 * rows, half), (rows, half)],
        [queries, codes, exps],
        [pltpu.HBM] * 3,
        [
            pltpu.VMEM((4, rows, half), codes.dtype),
            pltpu.VMEM(exps.shape, exps.dtype),
            pltpu.SemaphoreType.DMA((7,)),
        ],
    )


def lane_groups(heads):
    lane = lax.broadcasted_iota(jnp.int32, (1, HEAD_DIM), 1)
    return [(lane >= group * heads) & (lane < (group + 1) * heads) for group in range(2 * SPLIT_TERMS)], lane


def pack_stats(maxima, totals):
    heads = len(maxima)
    groups, lane = lane_groups(heads)
    is_maximum = lane < SPLIT_TERMS * heads
    left = jnp.zeros((maxima[0].shape[0], HEAD_DIM), jnp.float32)
    for head in range(heads):
        here = lane == head
        for group in range(1, 2 * SPLIT_TERMS):
            here = here | (lane == head + group * heads)
        left = jnp.where(here, jnp.where(is_maximum, maxima[head], totals[head]), left)
    packed = jnp.zeros_like(left)
    for term in range(SPLIT_TERMS):
        rounded = left.astype(jnp.bfloat16).astype(jnp.float32)
        packed = jnp.where(groups[term] | groups[SPLIT_TERMS + term], rounded, packed)
        left = left - rounded
    return packed.astype(jnp.bfloat16)


def unpack_stats(packed, heads):
    terms = packed.astype(jnp.float32)
    summed = terms
    for term in range(1, SPLIT_TERMS):
        summed = summed + pltpu.roll(terms, HEAD_DIM - term * heads, 1)
    return summed, pltpu.roll(summed, HEAD_DIM - SPLIT_TERMS * heads, 1)


def attend_kernel(stale_ref, query_parts, key_value_parts, out_refs):
    rows = query_parts[0].shape[0]
    width = query_parts[0].shape[1]
    patch = lax.axis_index("patch")
    uly = lax.axis_index("uly")
    heads = range(width // HEAD_DIM)

    def refreshed(kind):
        parts = []
        for block, part_ref in enumerate(key_value_parts):
            home = (patch ^ (block >> 1)) * 2 + (uly ^ (block & 1))
            stale = stale_ref[kind, pl.ds(pl.multiple_of(home * rows, rows), rows), :]
            parts.append(refresh(stale, part_ref[kind * rows : (kind + 1) * rows, :]))
        return jnp.concatenate(parts, axis=0)

    query_rows = jnp.concatenate([part_ref[...] for part_ref in query_parts], axis=0)
    key_rows = refreshed(0)
    scores = [head_scores(query_rows, key_rows, head) for head in heads]
    value_rows = refreshed(1)
    maxima = [jnp.max(each, axis=1, keepdims=True) for each in scores]
    weights = [jnp.exp(each - maximum) for each, maximum in zip(scores, maxima)]
    sums = [weigh_values(weights[head], value_rows, head) for head in heads]
    totals = [jnp.sum(each, axis=1, keepdims=True) for each in weights]
    for head in heads:
        result = (sums[head] / totals[head]).astype(jnp.bfloat16)
        for block, out_ref in enumerate(out_refs):
            out_ref[:, head * HEAD_DIM : (head + 1) * HEAD_DIM] = result[block * rows : (block + 1) * rows]
    stats = pack_stats(maxima, totals)
    for block, out_ref in enumerate(out_refs):
        out_ref[:, width : width + HEAD_DIM] = stats[block * rows : (block + 1) * rows]


def attend_partly(home, home_queries, beside, near, far_queries, own_stale):
    rows, width = home_queries.shape

    def body(home_ref, home_queries_ref, beside_ref, same_ref, diagonal_ref, far_ref, far_beside_ref, stale_ref, *out_refs):
        own_columns = aligned(lax.axis_index("uly") * width, width)
        query_parts = (
            home_queries_ref,
            beside_ref.at[pl.ds(2 * rows, rows)],
            far_ref.at[:, own_columns],
            far_beside_ref,
        )
        attend_kernel(stale_ref, query_parts, (home_ref, beside_ref, same_ref, diagonal_ref), out_refs)

    operands = [home, home_queries, beside, *near, *far_queries, own_stale]
    return kernel_call(body, [(rows, width + HEAD_DIM)] * 4, operands, [pltpu.VMEM] * len(operands))


def merge_kernel(part_refs, mixed_hbm, mixed_ref, sems):
    rows, packed_width = part_refs[0].shape
    width = packed_width - HEAD_DIM
    heads = width // HEAD_DIM
    uly = lax.axis_index("uly")
    stats = [unpack_stats(part_ref[:, width:], heads) for part_ref in part_refs]
    used = lax.broadcasted_iota(jnp.int32, (1, HEAD_DIM), 1) < heads
    shares = []
    for near, far in ((0, 2), (1, 3)):
        top = jnp.maximum(stats[near][0], stats[far][0])
        near_total = stats[near][1] * jnp.exp(stats[near][0] - top)
        far_total = stats[far][1] * jnp.exp(stats[far][0] - top)
        share = jnp.where(used, near_total / (near_total + far_total), 0.0)
        high = share.astype(jnp.bfloat16)
        shares += [high, (share - high.astype(jnp.float32)).astype(jnp.bfloat16)]
    head_of = lax.broadcasted_iota(jnp.int32, (HEAD_DIM, width), 1) // HEAD_DIM
    spread = (lax.broadcasted_iota(jnp.int32, (HEAD_DIM, width), 0) == head_of).astype(jnp.float32).astype(jnp.bfloat16)
    wide = jnp.dot(jnp.concatenate(shares, axis=0), spread, preferred_element_type=jnp.float32)
    copies = []
    for side, (near, far) in enumerate(((0, 2), (1, 3))):
        share = wide[2 * side * rows : (2 * side + 1) * rows] + wide[(2 * side + 1) * rows : (2 * side + 2) * rows]
        far_rows = part_refs[far][:, :width].astype(jnp.float32)
        near_rows = part_refs[near][:, :width].astype(jnp.float32)
        mixed_ref[side] = (far_rows + (near_rows - far_rows) * share).astype(jnp.bfloat16)
        columns = aligned((uly if side == 0 else 1 - uly) * width, width)
        copies.append(pltpu.make_async_copy(mixed_ref.at[side], mixed_hbm.at[:, columns], sems.at[side]))
        copies[side].start()
    for copy in copies:
        copy.wait()


def merge(parts):
    rows, packed_width = parts[0].shape
    width = packed_width - HEAD_DIM
    names = (0, *RETURN_ORDER)

    def body(*refs):
        named = dict(zip(names, refs))
        merge_kernel([named[block] for block in range(4)], *refs[4:])

    (mixed,) = kernel_call(
        body,
        [(rows, 2 * width)],
        [parts[name] for name in names],
        [pltpu.VMEM] * 4,
        [pltpu.VMEM((2, rows, width), jnp.bfloat16), pltpu.SemaphoreType.DMA((2,))],
        out_space=pltpu.HBM,
    )
    return mixed


def swap(array, distance):
    count = lax.axis_size(BOTH)
    return lax.ppermute(array, BOTH, [(peer, peer ^ distance) for peer in range(count)])


def attend_paired(queries, stale_kv, codes, exps):
    kv_rows = 2 * queries.shape[0]
    half = stale_kv.shape[2]
    far = swap(queries, 4)
    away, home, home_queries = decode_halves(queries, codes, exps)
    home, stale_kv = lax.optimization_barrier((home, stale_kv))
    own_stale = jnp.swapaxes(stale_kv, 0, 1)
    beside = swap(away, 1)
    near = [swap(home, 2), swap(away[:kv_rows], 3)]
    handed = lax.dynamic_slice(far, (0, (1 - lax.axis_index("uly")) * half), (far.shape[0], half))
    far_queries = [far, swap(handed, 1)]
    parts = attend_partly(home, home_queries, beside, near, far_queries, own_stale)
    return merge([parts[0]] + [swap(part, distance) for part, distance in zip(parts[1:], (1, 4, 5))])


def on_device(queries, stale_kv, codes, exps):
    if lax.axis_size("patch") == 4 and lax.axis_size("uly") == 2:
        return attend_paired(queries, stale_kv, codes, exps)
    return attend_gathered(queries, stale_kv, codes, exps)


def solution(mesh):
    return jax.shard_map(
        on_device,
        mesh=mesh,
        in_specs=(
            P(("rep", "patch", "uly"), None),
            P("rep", None, "uly"),
            P(("rep", "patch", "uly"), None, None),
            P(("rep", "patch", "uly"), None, None),
        ),
        out_specs=P(("rep", "patch", "uly"), None),
        check_vma=False,
    )
```

```python
import functools
import math

import jax
import jax.numpy as jnp
from jax import lax
from jax.experimental import pallas as pl
from jax.experimental.pallas import tpu as pltpu
from jax.sharding import PartitionSpec as P

HEAD_DIM = 128
SCALE_BLOCK = 128
KERNEL_VMEM = 8 << 20
BOTH = ("patch", "uly")
RETURN_ORDER = (3, 1, 2)
SPLIT_TERMS = 3
KEY, QUERY = 0, 1
FAR_QUERY_PARITY = 1


def decode(codes, exps):
    num_rows = codes.shape[0]
    num_blocks = exps.shape[2]
    scaled = (
        codes.astype(jnp.float32).reshape(num_rows, 2, num_blocks, SCALE_BLOCK)
        * jnp.exp2(exps.astype(jnp.float32))[..., None]
    )
    return scaled.reshape(num_rows, 2, num_blocks * SCALE_BLOCK).astype(jnp.bfloat16)


def refresh(stale_part, resid_part):
    return (stale_part.astype(jnp.float32) + resid_part.astype(jnp.float32)).astype(jnp.bfloat16)


def column_block(rows, head):
    return rows[:, head * HEAD_DIM : (head + 1) * HEAD_DIM]


def head_scores(query_rows, key_rows, head):
    scores = lax.dot_general(
        column_block(query_rows, head),
        column_block(key_rows, head),
        (((1,), (1,)), ((), ())),
        preferred_element_type=jnp.float32,
    )
    return scores * (1.0 / math.sqrt(HEAD_DIM))


def weigh_values(weights, value_rows, head):
    return jnp.dot(
        weights.astype(jnp.bfloat16),
        column_block(value_rows, head),
        preferred_element_type=jnp.float32,
    )


def attend_whole(query_rows, kv_rows):
    head_count = query_rows.shape[1] // HEAD_DIM
    key_rows = kv_rows[:, 0]
    value_rows = kv_rows[:, 1]
    outputs = []
    for head in range(head_count):
        scores = head_scores(query_rows, key_rows, head)
        row_max = jnp.max(scores, axis=1, keepdims=True)
        weights = jnp.exp(scores - row_max)
        totals = jnp.sum(weights, axis=1, keepdims=True)
        outputs.append(weigh_values(weights, value_rows, head) / totals)
    return jnp.concatenate(outputs, axis=1).astype(jnp.bfloat16)


def attend_gathered(queries, stale_kv, codes, exps):
    residual = decode(codes, exps)
    query_rows = lax.all_to_all(queries, "uly", split_axis=1, concat_axis=0, tiled=True)
    gathered = lax.all_gather(residual, "patch", axis=0, tiled=True)
    patch_count = lax.axis_size("patch")
    blocked = gathered.reshape(patch_count, residual.shape[0], 2, residual.shape[2])
    spread = lax.all_to_all(blocked, "uly", split_axis=3, concat_axis=1, tiled=True)
    all_resid = spread.reshape(stale_kv.shape)
    result = attend_whole(query_rows, refresh(stale_kv, all_resid))
    return lax.all_to_all(result, "uly", split_axis=0, concat_axis=1, tiled=True)


def aligned(start, size):
    return pl.ds(pl.multiple_of(start, HEAD_DIM), size)


def kernel_call(body, outputs, operands, spaces, scratch=(), out_space=pltpu.VMEM):
    operands = [
        pltpu.with_memory_space_constraint(each, pltpu.HBM) if space is pltpu.HBM else each
        for each, space in zip(operands, spaces)
    ]
    return pl.pallas_call(
        body,
        out_shape=[jax.ShapeDtypeStruct(shape, jnp.bfloat16) for shape in outputs],
        in_specs=[pl.BlockSpec(memory_space=space) for space in spaces],
        out_specs=[pl.BlockSpec(memory_space=out_space)] * len(outputs),
        scratch_shapes=list(scratch),
        compiler_params=pltpu.CompilerParams(vmem_limit_bytes=KERNEL_VMEM),
    )(*operands)


def decode_kernel(queries_hbm, codes_hbm, exps_hbm, away_ref, home_ref, home_queries_ref, codes_ref, exps_ref, sems):
    rows, half = home_queries_ref.shape
    uly = lax.axis_index("uly")
    starts = ((1 - uly) * half, uly * half)
    fetch_exps = pltpu.make_async_copy(exps_hbm, exps_ref, sems.at[0])
    fetch_exps.start()
    fetch_codes = []
    for start in starts:
        for kind in range(2):
            slot = len(fetch_codes)
            fetch_codes.append(
                pltpu.make_async_copy(codes_hbm.at[:, kind, aligned(start, half)], codes_ref.at[slot], sems.at[1 + slot])
            )
            fetch_codes[slot].start()
    fetch_queries = []
    for side, target in enumerate((away_ref.at[pl.ds(2 * rows, rows)], home_queries_ref)):
        fetch_queries.append(pltpu.make_async_copy(queries_hbm.at[:, aligned(starts[side], half)], target, sems.at[5 + side]))
        fetch_queries[side].start()
    blocks = exps_ref.shape[2]
    block_of = lax.broadcasted_iota(jnp.int32, (blocks, half), 1) // SCALE_BLOCK
    row_of = lax.broadcasted_iota(jnp.int32, (blocks, half), 0)
    fetch_exps.wait()
    scales = jnp.concatenate([jnp.exp2(exps_ref[:, kind, :].astype(jnp.float32)) for kind in range(2)], axis=0)
    scales = scales.astype(jnp.bfloat16)
    spreads = [(row_of == block_of + start // SCALE_BLOCK).astype(jnp.float32).astype(jnp.bfloat16) for start in starts]
    wide_scales = [jnp.dot(scales, spread, preferred_element_type=jnp.float32) for spread in spreads]
    for side, out_ref in enumerate((away_ref, home_ref)):
        for kind in range(2):
            fetch_codes[2 * side + kind].wait()
            own_rows = slice(kind * rows, (kind + 1) * rows)
            decoded = codes_ref[2 * side + kind].astype(jnp.float32) * wide_scales[side][own_rows]
            out_ref[own_rows, :] = decoded.astype(jnp.bfloat16)
    for fetch in fetch_queries:
        fetch.wait()


def decode_halves(queries, codes, exps):
    rows, model_width = queries.shape
    half = model_width // lax.axis_size("uly")
    return kernel_call(
        decode_kernel,
        [(3 * rows, half), (2 * rows, half), (rows, half)],
        [queries, codes, exps],
        [pltpu.HBM] * 3,
        [
            pltpu.VMEM((4, rows, half), codes.dtype),
            pltpu.VMEM(exps.shape, exps.dtype),
            pltpu.SemaphoreType.DMA((7,)),
        ],
    )


def lane_groups(heads):
    lane = lax.broadcasted_iota(jnp.int32, (1, HEAD_DIM), 1)
    return [(lane >= group * heads) & (lane < (group + 1) * heads) for group in range(2 * SPLIT_TERMS)], lane


def pack_stats(maxima, totals):
    heads = len(maxima)
    groups, lane = lane_groups(heads)
    is_maximum = lane < SPLIT_TERMS * heads
    left = jnp.zeros((maxima[0].shape[0], HEAD_DIM), jnp.float32)
    for head in range(heads):
        here = lane == head
        for group in range(1, 2 * SPLIT_TERMS):
            here = here | (lane == head + group * heads)
        left = jnp.where(here, jnp.where(is_maximum, maxima[head], totals[head]), left)
    packed = jnp.zeros_like(left)
    for term in range(SPLIT_TERMS):
        rounded = left.astype(jnp.bfloat16).astype(jnp.float32)
        packed = jnp.where(groups[term] | groups[SPLIT_TERMS + term], rounded, packed)
        left = left - rounded
    return packed.astype(jnp.bfloat16)


def unpack_stats(packed, heads):
    terms = packed.astype(jnp.float32)
    summed = terms
    for term in range(1, SPLIT_TERMS):
        summed = summed + pltpu.roll(terms, HEAD_DIM - term * heads, 1)
    return summed, pltpu.roll(summed, HEAD_DIM - SPLIT_TERMS * heads, 1)


def attend_kernel(stale_ref, query_parts, key_value_parts, out_refs):
    rows = query_parts[0].shape[0]
    width = query_parts[0].shape[1]
    patch = lax.axis_index("patch")
    uly = lax.axis_index("uly")
    odd = lax.rem(lax.axis_index("rep"), 2)
    key_step = steps_of(0)[KEY] + odd * (steps_of(1)[KEY] - steps_of(0)[KEY])
    heads = range(width // HEAD_DIM)

    def refreshed(kind):
        parts = []
        for block, part_ref in enumerate(key_value_parts):
            home = (patch ^ ((block >> 1) * key_step)) * 2 + (uly ^ (block & 1))
            stale = stale_ref[kind, pl.ds(pl.multiple_of(home * rows, rows), rows), :]
            parts.append(refresh(stale, part_ref[kind * rows : (kind + 1) * rows, :]))
        return jnp.concatenate(parts, axis=0)

    query_rows = jnp.concatenate([part_ref[...] for part_ref in query_parts], axis=0)
    key_rows = refreshed(0)
    scores = [head_scores(query_rows, key_rows, head) for head in heads]
    value_rows = refreshed(1)
    maxima = [jnp.max(each, axis=1, keepdims=True) for each in scores]
    weights = [jnp.exp(each - maximum) for each, maximum in zip(scores, maxima)]
    sums = [weigh_values(weights[head], value_rows, head) for head in heads]
    totals = [jnp.sum(each, axis=1, keepdims=True) for each in weights]
    for head in heads:
        result = (sums[head] / totals[head]).astype(jnp.bfloat16)
        for block, out_ref in enumerate(out_refs):
            out_ref[:, head * HEAD_DIM : (head + 1) * HEAD_DIM] = result[block * rows : (block + 1) * rows]
    stats = pack_stats(maxima, totals)
    for block, out_ref in enumerate(out_refs):
        out_ref[:, width : width + HEAD_DIM] = stats[block * rows : (block + 1) * rows]


def attend_partly(home, home_queries, beside, near, far_queries, own_stale):
    rows, width = home_queries.shape

    def body(home_ref, home_queries_ref, beside_ref, same_ref, diagonal_ref, far_ref, far_beside_ref, stale_ref, *out_refs):
        own_columns = aligned(lax.axis_index("uly") * width, width)
        query_parts = (
            home_queries_ref,
            beside_ref.at[pl.ds(2 * rows, rows)],
            far_ref.at[:, own_columns],
            far_beside_ref,
        )
        attend_kernel(stale_ref, query_parts, (home_ref, beside_ref, same_ref, diagonal_ref), out_refs)

    operands = [home, home_queries, beside, *near, *far_queries, own_stale]
    return kernel_call(body, [(rows, width + HEAD_DIM)] * 4, operands, [pltpu.VMEM] * len(operands))


def merge_kernel(part_refs, mixed_hbm, mixed_ref, sems):
    rows, packed_width = part_refs[0].shape
    width = packed_width - HEAD_DIM
    heads = width // HEAD_DIM
    uly = lax.axis_index("uly")
    stats = [unpack_stats(part_ref[:, width:], heads) for part_ref in part_refs]
    used = lax.broadcasted_iota(jnp.int32, (1, HEAD_DIM), 1) < heads
    shares = []
    for near, far in ((0, 2), (1, 3)):
        top = jnp.maximum(stats[near][0], stats[far][0])
        near_total = stats[near][1] * jnp.exp(stats[near][0] - top)
        far_total = stats[far][1] * jnp.exp(stats[far][0] - top)
        share = jnp.where(used, near_total / (near_total + far_total), 0.0)
        high = share.astype(jnp.bfloat16)
        shares += [high, (share - high.astype(jnp.float32)).astype(jnp.bfloat16)]
    head_of = lax.broadcasted_iota(jnp.int32, (HEAD_DIM, width), 1) // HEAD_DIM
    spread = (lax.broadcasted_iota(jnp.int32, (HEAD_DIM, width), 0) == head_of).astype(jnp.float32).astype(jnp.bfloat16)
    wide = jnp.dot(jnp.concatenate(shares, axis=0), spread, preferred_element_type=jnp.float32)
    copies = []
    for side, (near, far) in enumerate(((0, 2), (1, 3))):
        share = wide[2 * side * rows : (2 * side + 1) * rows] + wide[(2 * side + 1) * rows : (2 * side + 2) * rows]
        far_rows = part_refs[far][:, :width].astype(jnp.float32)
        near_rows = part_refs[near][:, :width].astype(jnp.float32)
        mixed_ref[side] = (far_rows + (near_rows - far_rows) * share).astype(jnp.bfloat16)
        columns = aligned((uly if side == 0 else 1 - uly) * width, width)
        copies.append(pltpu.make_async_copy(mixed_ref.at[side], mixed_hbm.at[:, columns], sems.at[side]))
        copies[side].start()
    for copy in copies:
        copy.wait()


def merge(parts):
    rows, packed_width = parts[0].shape
    width = packed_width - HEAD_DIM
    names = (0, *RETURN_ORDER)

    def body(*refs):
        named = dict(zip(names, refs))
        merge_kernel([named[block] for block in range(4)], *refs[4:])

    (mixed,) = kernel_call(
        body,
        [(rows, 2 * width)],
        [parts[name] for name in names],
        [pltpu.VMEM] * 4,
        [pltpu.VMEM((2, rows, width), jnp.bfloat16), pltpu.SemaphoreType.DMA((2,))],
        out_space=pltpu.HBM,
    )
    return mixed


def steps_of(rep):
    return (1, 2) if rep % 2 == FAR_QUERY_PARITY else (2, 1)


def swap(array, role, uly):
    peers = lax.axis_size(BOTH)
    pairs = []
    reps = lax.axis_size("rep")
    for rep in range(reps):
        step = 0 if role is None else steps_of(rep)[role]
        pairs += [(peer * reps + rep, (peer ^ (2 * step + uly)) * reps + rep) for peer in range(peers)]
    return lax.ppermute(array, (*BOTH, "rep"), pairs)


def attend_paired(queries, stale_kv, codes, exps):
    kv_rows = 2 * queries.shape[0]
    half = stale_kv.shape[2]
    far = swap(queries, QUERY, 0)
    away, home, home_queries = decode_halves(queries, codes, exps)
    home, stale_kv = lax.optimization_barrier((home, stale_kv))
    own_stale = jnp.swapaxes(stale_kv, 0, 1)
    beside = swap(away, None, 1)
    near = [swap(home, KEY, 0), swap(away[:kv_rows], KEY, 1)]
    handed = lax.dynamic_slice(far, (0, (1 - lax.axis_index("uly")) * half), (far.shape[0], half))
    far_queries = [far, swap(handed, None, 1)]
    parts = attend_partly(home, home_queries, beside, near, far_queries, own_stale)
    homes = ((None, 1), (QUERY, 0), (QUERY, 1))
    return merge([parts[0]] + [swap(part, *home) for part, home in zip(parts[1:], homes)])


def on_device(queries, stale_kv, codes, exps):
    if lax.axis_size("patch") == 4 and lax.axis_size("uly") == 2:
        return attend_paired(queries, stale_kv, codes, exps)
    return attend_gathered(queries, stale_kv, codes, exps)


def solution(mesh):
    return jax.shard_map(
        on_device,
        mesh=mesh,
        in_specs=(
            P(("rep", "patch", "uly"), None),
            P("rep", None, "uly"),
            P(("rep", "patch", "uly"), None, None),
            P(("rep", "patch", "uly"), None, None),
        ),
        out_specs=P(("rep", "patch", "uly"), None),
        check_vma=False,
    )
```

```python
import functools
import math

import jax
import jax.numpy as jnp
from jax import lax
from jax.experimental import pallas as pl
from jax.experimental.pallas import tpu as pltpu
from jax.sharding import PartitionSpec as P

HEAD_DIM = 128
SCALE_BLOCK = 128
KERNEL_VMEM = 8 << 20
BOTH = ("patch", "uly")
RETURN_ORDER = (3, 1, 2)
SPLIT_TERMS = 3
KEY_VALUE_ORDER = (2, 3, 1)
KEY, QUERY = 0, 1
FAR_QUERY_PARITY = 1


def decode(codes, exps):
    num_rows = codes.shape[0]
    num_blocks = exps.shape[2]
    scaled = (
        codes.astype(jnp.float32).reshape(num_rows, 2, num_blocks, SCALE_BLOCK)
        * jnp.exp2(exps.astype(jnp.float32))[..., None]
    )
    return scaled.reshape(num_rows, 2, num_blocks * SCALE_BLOCK).astype(jnp.bfloat16)


def refresh(stale_part, resid_part):
    return (stale_part.astype(jnp.float32) + resid_part.astype(jnp.float32)).astype(jnp.bfloat16)


def column_block(rows, head):
    return rows[:, head * HEAD_DIM : (head + 1) * HEAD_DIM]


def head_scores(query_rows, key_rows, head):
    scores = lax.dot_general(
        column_block(query_rows, head),
        column_block(key_rows, head),
        (((1,), (1,)), ((), ())),
        preferred_element_type=jnp.float32,
    )
    return scores * (1.0 / math.sqrt(HEAD_DIM))


def weigh_values(weights, value_rows, head):
    return jnp.dot(
        weights.astype(jnp.bfloat16),
        column_block(value_rows, head),
        preferred_element_type=jnp.float32,
    )


def attend_whole(query_rows, kv_rows):
    head_count = query_rows.shape[1] // HEAD_DIM
    key_rows = kv_rows[:, 0]
    value_rows = kv_rows[:, 1]
    outputs = []
    for head in range(head_count):
        scores = head_scores(query_rows, key_rows, head)
        row_max = jnp.max(scores, axis=1, keepdims=True)
        weights = jnp.exp(scores - row_max)
        totals = jnp.sum(weights, axis=1, keepdims=True)
        outputs.append(weigh_values(weights, value_rows, head) / totals)
    return jnp.concatenate(outputs, axis=1).astype(jnp.bfloat16)


def attend_gathered(queries, stale_kv, codes, exps):
    residual = decode(codes, exps)
    query_rows = lax.all_to_all(queries, "uly", split_axis=1, concat_axis=0, tiled=True)
    gathered = lax.all_gather(residual, "patch", axis=0, tiled=True)
    patch_count = lax.axis_size("patch")
    blocked = gathered.reshape(patch_count, residual.shape[0], 2, residual.shape[2])
    spread = lax.all_to_all(blocked, "uly", split_axis=3, concat_axis=1, tiled=True)
    all_resid = spread.reshape(stale_kv.shape)
    result = attend_whole(query_rows, refresh(stale_kv, all_resid))
    return lax.all_to_all(result, "uly", split_axis=0, concat_axis=1, tiled=True)


def aligned(start, size):
    return pl.ds(pl.multiple_of(start, HEAD_DIM), size)


def kernel_call(body, outputs, operands, spaces, scratch=(), out_space=pltpu.VMEM):
    operands = [
        pltpu.with_memory_space_constraint(each, pltpu.HBM) if space is pltpu.HBM else each
        for each, space in zip(operands, spaces)
    ]
    return pl.pallas_call(
        body,
        out_shape=[jax.ShapeDtypeStruct(shape, jnp.bfloat16) for shape in outputs],
        in_specs=[pl.BlockSpec(memory_space=space) for space in spaces],
        out_specs=[pl.BlockSpec(memory_space=out_space)] * len(outputs),
        scratch_shapes=list(scratch),
        compiler_params=pltpu.CompilerParams(vmem_limit_bytes=KERNEL_VMEM),
    )(*operands)


def decode_kernel(
    queries_hbm, codes_hbm, exps_hbm, away_ref, home_ref, away_queries_ref, home_queries_ref, codes_ref, exps_ref, sems
):
    rows, half = home_queries_ref.shape
    uly = lax.axis_index("uly")
    starts = ((1 - uly) * half, uly * half)
    fetch_exps = pltpu.make_async_copy(exps_hbm, exps_ref, sems.at[0])
    fetch_exps.start()
    fetch_codes = []
    for start in starts:
        for kind in range(2):
            slot = len(fetch_codes)
            fetch_codes.append(
                pltpu.make_async_copy(codes_hbm.at[:, kind, aligned(start, half)], codes_ref.at[slot], sems.at[1 + slot])
            )
            fetch_codes[slot].start()
    fetch_queries = []
    for side, target in enumerate((away_queries_ref, home_queries_ref)):
        fetch_queries.append(pltpu.make_async_copy(queries_hbm.at[:, aligned(starts[side], half)], target, sems.at[5 + side]))
        fetch_queries[side].start()
    blocks = exps_ref.shape[2]
    block_of = lax.broadcasted_iota(jnp.int32, (blocks, half), 1) // SCALE_BLOCK
    row_of = lax.broadcasted_iota(jnp.int32, (blocks, half), 0)
    fetch_exps.wait()
    scales = jnp.concatenate([jnp.exp2(exps_ref[:, kind, :].astype(jnp.float32)) for kind in range(2)], axis=0)
    scales = scales.astype(jnp.bfloat16)
    spreads = [(row_of == block_of + start // SCALE_BLOCK).astype(jnp.float32).astype(jnp.bfloat16) for start in starts]
    wide_scales = [jnp.dot(scales, spread, preferred_element_type=jnp.float32) for spread in spreads]
    for side, out_ref in enumerate((away_ref, home_ref)):
        for kind in range(2):
            fetch_codes[2 * side + kind].wait()
            own_rows = slice(kind * rows, (kind + 1) * rows)
            decoded = codes_ref[2 * side + kind].astype(jnp.float32) * wide_scales[side][own_rows]
            out_ref[own_rows, :] = decoded.astype(jnp.bfloat16)
    for fetch in fetch_queries:
        fetch.wait()


def decode_halves(queries, codes, exps):
    rows, model_width = queries.shape
    half = model_width // lax.axis_size("uly")
    return kernel_call(
        decode_kernel,
        [(2 * rows, half)] * 2 + [(rows, half)] * 2,
        [queries, codes, exps],
        [pltpu.HBM] * 3,
        [
            pltpu.VMEM((4, rows, half), codes.dtype),
            pltpu.VMEM(exps.shape, exps.dtype),
            pltpu.SemaphoreType.DMA((7,)),
        ],
    )


def lane_groups(heads):
    lane = lax.broadcasted_iota(jnp.int32, (1, HEAD_DIM), 1)
    return [(lane >= group * heads) & (lane < (group + 1) * heads) for group in range(2 * SPLIT_TERMS)], lane


def pack_stats(maxima, totals):
    heads = len(maxima)
    groups, lane = lane_groups(heads)
    is_maximum = lane < SPLIT_TERMS * heads
    left = jnp.zeros((maxima[0].shape[0], HEAD_DIM), jnp.float32)
    for head in range(heads):
        here = lane == head
        for group in range(1, 2 * SPLIT_TERMS):
            here = here | (lane == head + group * heads)
        left = jnp.where(here, jnp.where(is_maximum, maxima[head], totals[head]), left)
    packed = jnp.zeros_like(left)
    for term in range(SPLIT_TERMS):
        rounded = left.astype(jnp.bfloat16).astype(jnp.float32)
        packed = jnp.where(groups[term] | groups[SPLIT_TERMS + term], rounded, packed)
        left = left - rounded
    return packed.astype(jnp.bfloat16)


def unpack_stats(packed, heads):
    terms = packed.astype(jnp.float32)
    summed = terms
    for term in range(1, SPLIT_TERMS):
        summed = summed + pltpu.roll(terms, HEAD_DIM - term * heads, 1)
    return summed, pltpu.roll(summed, HEAD_DIM - SPLIT_TERMS * heads, 1)


def attend_kernel(stale_ref, query_parts, key_value_parts, out_refs):
    rows = query_parts[0].shape[0]
    width = query_parts[0].shape[1]
    patch = lax.axis_index("patch")
    uly = lax.axis_index("uly")
    odd = lax.rem(lax.axis_index("rep"), 2)
    key_step = steps_of(0)[KEY] + odd * (steps_of(1)[KEY] - steps_of(0)[KEY])
    heads = range(width // HEAD_DIM)

    def refreshed(kind):
        parts = []
        for block, part_ref in enumerate(key_value_parts):
            home = (patch ^ ((block >> 1) * key_step)) * 2 + (uly ^ (block & 1))
            stale = stale_ref[kind, pl.ds(pl.multiple_of(home * rows, rows), rows), :]
            parts.append(refresh(stale, part_ref[kind * rows : (kind + 1) * rows, :]))
        return jnp.concatenate(parts, axis=0)

    query_rows = jnp.concatenate([part_ref[...] for part_ref in query_parts], axis=0)
    key_rows = refreshed(0)
    scores = [head_scores(query_rows, key_rows, head) for head in heads]
    value_rows = refreshed(1)
    maxima = [jnp.max(each, axis=1, keepdims=True) for each in scores]
    weights = [jnp.exp(each - maximum) for each, maximum in zip(scores, maxima)]
    sums = [weigh_values(weights[head], value_rows, head) for head in heads]
    totals = [jnp.sum(each, axis=1, keepdims=True) for each in weights]
    for head in heads:
        result = (sums[head] / totals[head]).astype(jnp.bfloat16)
        for block, out_ref in enumerate(out_refs):
            out_ref[:, head * HEAD_DIM : (head + 1) * HEAD_DIM] = result[block * rows : (block + 1) * rows]
    stats = pack_stats(maxima, totals)
    for block, out_ref in enumerate(out_refs):
        out_ref[:, width : width + HEAD_DIM] = stats[block * rows : (block + 1) * rows]


def attend_partly(home, home_queries, key_values, other_queries, handed, own_stale):
    rows, width = home_queries.shape

    def body(home_ref, home_queries_ref, *refs):
        named = dict(zip(KEY_VALUE_ORDER, refs))
        other_ref, handed_ref, stale_ref, *out_refs = refs[len(KEY_VALUE_ORDER) :]
        own_columns = aligned(lax.axis_index("uly") * width, width)
        query_parts = (home_queries_ref, handed_ref.at[0], other_ref.at[:, own_columns], handed_ref.at[1])
        attend_kernel(stale_ref, query_parts, (home_ref, *(named[block] for block in (1, 2, 3))), out_refs)

    operands = [home, home_queries, *(key_values[block] for block in KEY_VALUE_ORDER), other_queries, handed, own_stale]
    return kernel_call(body, [(rows, width + HEAD_DIM)] * 4, operands, [pltpu.VMEM] * len(operands))


def merge_kernel(part_refs, mixed_hbm, mixed_ref, sems):
    rows, packed_width = part_refs[0].shape
    width = packed_width - HEAD_DIM
    heads = width // HEAD_DIM
    uly = lax.axis_index("uly")
    stats = [unpack_stats(part_ref[:, width:], heads) for part_ref in part_refs]
    used = lax.broadcasted_iota(jnp.int32, (1, HEAD_DIM), 1) < heads
    shares = []
    for near, far in ((0, 2), (1, 3)):
        top = jnp.maximum(stats[near][0], stats[far][0])
        near_total = stats[near][1] * jnp.exp(stats[near][0] - top)
        far_total = stats[far][1] * jnp.exp(stats[far][0] - top)
        share = jnp.where(used, near_total / (near_total + far_total), 0.0)
        high = share.astype(jnp.bfloat16)
        shares += [high, (share - high.astype(jnp.float32)).astype(jnp.bfloat16)]
    head_of = lax.broadcasted_iota(jnp.int32, (HEAD_DIM, width), 1) // HEAD_DIM
    spread = (lax.broadcasted_iota(jnp.int32, (HEAD_DIM, width), 0) == head_of).astype(jnp.float32).astype(jnp.bfloat16)
    wide = jnp.dot(jnp.concatenate(shares, axis=0), spread, preferred_element_type=jnp.float32)
    copies = []
    for side, (near, far) in enumerate(((0, 2), (1, 3))):
        share = wide[2 * side * rows : (2 * side + 1) * rows] + wide[(2 * side + 1) * rows : (2 * side + 2) * rows]
        far_rows = part_refs[far][:, :width].astype(jnp.float32)
        near_rows = part_refs[near][:, :width].astype(jnp.float32)
        mixed_ref[side] = (far_rows + (near_rows - far_rows) * share).astype(jnp.bfloat16)
        columns = aligned((uly if side == 0 else 1 - uly) * width, width)
        copies.append(pltpu.make_async_copy(mixed_ref.at[side], mixed_hbm.at[:, columns], sems.at[side]))
        copies[side].start()
    for copy in copies:
        copy.wait()


def merge(parts):
    rows, packed_width = parts[0].shape
    width = packed_width - HEAD_DIM
    names = (0, *RETURN_ORDER)

    def body(*refs):
        named = dict(zip(names, refs))
        merge_kernel([named[block] for block in range(4)], *refs[4:])

    (mixed,) = kernel_call(
        body,
        [(rows, 2 * width)],
        [parts[name] for name in names],
        [pltpu.VMEM] * 4,
        [pltpu.VMEM((2, rows, width), jnp.bfloat16), pltpu.SemaphoreType.DMA((2,))],
        out_space=pltpu.HBM,
    )
    return mixed


def steps_of(rep):
    return (1, 2) if rep % 2 == FAR_QUERY_PARITY else (2, 1)


def swap(array, role, uly):
    peers = lax.axis_size(BOTH)
    pairs = []
    reps = lax.axis_size("rep")
    for rep in range(reps):
        step = 0 if role is None else steps_of(rep)[role]
        pairs += [(peer * reps + rep, (peer ^ (2 * step + uly)) * reps + rep) for peer in range(peers)]
    return lax.ppermute(array, (*BOTH, "rep"), pairs)


def attend_paired(queries, stale_kv, codes, exps):
    half = stale_kv.shape[2]
    other = swap(queries, QUERY, 0)
    away, home, away_queries, home_queries = decode_halves(queries, codes, exps)
    home, stale_kv = lax.optimization_barrier((home, stale_kv))
    own_stale = jnp.swapaxes(stale_kv, 0, 1)
    key_values = {1: swap(away, None, 1), 2: swap(home, KEY, 0), 3: swap(away, KEY, 1)}
    other_away = lax.dynamic_slice(other, (0, (1 - lax.axis_index("uly")) * half), (other.shape[0], half))
    handed = swap(jnp.stack([away_queries, other_away]), None, 1)
    parts = attend_partly(home, home_queries, key_values, other, handed, own_stale)
    homes = ((None, 1), (QUERY, 0), (QUERY, 1))
    return merge([parts[0]] + [swap(part, *home) for part, home in zip(parts[1:], homes)])


def on_device(queries, stale_kv, codes, exps):
    if lax.axis_size("patch") == 4 and lax.axis_size("uly") == 2:
        return attend_paired(queries, stale_kv, codes, exps)
    return attend_gathered(queries, stale_kv, codes, exps)


def solution(mesh):
    return jax.shard_map(
        on_device,
        mesh=mesh,
        in_specs=(
            P(("rep", "patch", "uly"), None),
            P("rep", None, "uly"),
            P(("rep", "patch", "uly"), None, None),
            P(("rep", "patch", "uly"), None, None),
        ),
        out_specs=P(("rep", "patch", "uly"), None),
        check_vma=False,
    )
```

```python
import functools
import math

import jax
import jax.numpy as jnp
from jax import lax
from jax.experimental import pallas as pl
from jax.experimental.pallas import tpu as pltpu
from jax.sharding import PartitionSpec as P

HEAD_DIM = 128
SCALE_BLOCK = 128
KERNEL_VMEM = 8 << 20
BOTH = ("patch", "uly")
SPLIT_TERMS = 3
KEY_VALUE_ORDER = (3, 2, 1)
KEY, QUERY = 0, 1
FAR_QUERY_PARITY = 1


def decode(codes, exps):
    num_rows = codes.shape[0]
    num_blocks = exps.shape[2]
    scaled = (
        codes.astype(jnp.float32).reshape(num_rows, 2, num_blocks, SCALE_BLOCK)
        * jnp.exp2(exps.astype(jnp.float32))[..., None]
    )
    return scaled.reshape(num_rows, 2, num_blocks * SCALE_BLOCK).astype(jnp.bfloat16)


def refresh(stale_part, resid_part):
    return (stale_part.astype(jnp.float32) + resid_part.astype(jnp.float32)).astype(jnp.bfloat16)


def column_block(rows, head):
    return rows[:, head * HEAD_DIM : (head + 1) * HEAD_DIM]


def head_scores(query_rows, key_rows, head):
    scores = lax.dot_general(
        column_block(query_rows, head),
        column_block(key_rows, head),
        (((1,), (1,)), ((), ())),
        preferred_element_type=jnp.float32,
    )
    return scores * (1.0 / math.sqrt(HEAD_DIM))


def weigh_values(weights, value_rows, head):
    return jnp.dot(
        weights.astype(jnp.bfloat16),
        column_block(value_rows, head),
        preferred_element_type=jnp.float32,
    )


def attend_whole(query_rows, kv_rows):
    head_count = query_rows.shape[1] // HEAD_DIM
    key_rows = kv_rows[:, 0]
    value_rows = kv_rows[:, 1]
    outputs = []
    for head in range(head_count):
        scores = head_scores(query_rows, key_rows, head)
        row_max = jnp.max(scores, axis=1, keepdims=True)
        weights = jnp.exp(scores - row_max)
        totals = jnp.sum(weights, axis=1, keepdims=True)
        outputs.append(weigh_values(weights, value_rows, head) / totals)
    return jnp.concatenate(outputs, axis=1).astype(jnp.bfloat16)


def attend_gathered(queries, stale_kv, codes, exps):
    residual = decode(codes, exps)
    query_rows = lax.all_to_all(queries, "uly", split_axis=1, concat_axis=0, tiled=True)
    gathered = lax.all_gather(residual, "patch", axis=0, tiled=True)
    patch_count = lax.axis_size("patch")
    blocked = gathered.reshape(patch_count, residual.shape[0], 2, residual.shape[2])
    spread = lax.all_to_all(blocked, "uly", split_axis=3, concat_axis=1, tiled=True)
    all_resid = spread.reshape(stale_kv.shape)
    result = attend_whole(query_rows, refresh(stale_kv, all_resid))
    return lax.all_to_all(result, "uly", split_axis=0, concat_axis=1, tiled=True)


def aligned(start, size):
    return pl.ds(pl.multiple_of(start, HEAD_DIM), size)


def kernel_call(body, outputs, operands, spaces, scratch=(), out_space=pltpu.VMEM):
    operands = [
        pltpu.with_memory_space_constraint(each, pltpu.HBM) if space is pltpu.HBM else each
        for each, space in zip(operands, spaces)
    ]
    return pl.pallas_call(
        body,
        out_shape=[jax.ShapeDtypeStruct(shape, jnp.bfloat16) for shape in outputs],
        in_specs=[pl.BlockSpec(memory_space=space) for space in spaces],
        out_specs=[pl.BlockSpec(memory_space=out_space)] * len(outputs),
        scratch_shapes=list(scratch),
        compiler_params=pltpu.CompilerParams(vmem_limit_bytes=KERNEL_VMEM),
    )(*operands)


def decode_kernel(
    queries_hbm, codes_hbm, exps_hbm, away_ref, home_ref, away_queries_ref, home_queries_ref, codes_ref, exps_ref, sems
):
    rows, half = home_queries_ref.shape
    uly = lax.axis_index("uly")
    starts = ((1 - uly) * half, uly * half)
    fetch_exps = pltpu.make_async_copy(exps_hbm, exps_ref, sems.at[0])
    fetch_exps.start()
    fetch_codes = []
    for start in starts:
        for kind in range(2):
            slot = len(fetch_codes)
            fetch_codes.append(
                pltpu.make_async_copy(codes_hbm.at[:, kind, aligned(start, half)], codes_ref.at[slot], sems.at[1 + slot])
            )
            fetch_codes[slot].start()
    fetch_queries = []
    for side, target in enumerate((away_queries_ref, home_queries_ref)):
        fetch_queries.append(pltpu.make_async_copy(queries_hbm.at[:, aligned(starts[side], half)], target, sems.at[5 + side]))
        fetch_queries[side].start()
    blocks = exps_ref.shape[2]
    block_of = lax.broadcasted_iota(jnp.int32, (blocks, half), 1) // SCALE_BLOCK
    row_of = lax.broadcasted_iota(jnp.int32, (blocks, half), 0)
    fetch_exps.wait()
    scales = jnp.concatenate([jnp.exp2(exps_ref[:, kind, :].astype(jnp.float32)) for kind in range(2)], axis=0)
    scales = scales.astype(jnp.bfloat16)
    spreads = [(row_of == block_of + start // SCALE_BLOCK).astype(jnp.float32).astype(jnp.bfloat16) for start in starts]
    wide_scales = [jnp.dot(scales, spread, preferred_element_type=jnp.float32) for spread in spreads]
    for side, out_ref in enumerate((away_ref, home_ref)):
        for kind in range(2):
            fetch_codes[2 * side + kind].wait()
            own_rows = slice(kind * rows, (kind + 1) * rows)
            decoded = codes_ref[2 * side + kind].astype(jnp.float32) * wide_scales[side][own_rows]
            out_ref[own_rows, :] = decoded.astype(jnp.bfloat16)
    for fetch in fetch_queries:
        fetch.wait()


def decode_halves(queries, codes, exps):
    rows, model_width = queries.shape
    half = model_width // lax.axis_size("uly")
    return kernel_call(
        decode_kernel,
        [(2 * rows, half)] * 2 + [(rows, half)] * 2,
        [queries, codes, exps],
        [pltpu.HBM] * 3,
        [
            pltpu.VMEM((4, rows, half), codes.dtype),
            pltpu.VMEM(exps.shape, exps.dtype),
            pltpu.SemaphoreType.DMA((7,)),
        ],
    )


def lane_groups(heads):
    lane = lax.broadcasted_iota(jnp.int32, (1, HEAD_DIM), 1)
    return [(lane >= group * heads) & (lane < (group + 1) * heads) for group in range(2 * SPLIT_TERMS)], lane


def pack_stats(maxima, totals):
    heads = len(maxima)
    groups, lane = lane_groups(heads)
    is_maximum = lane < SPLIT_TERMS * heads
    left = jnp.zeros((maxima[0].shape[0], HEAD_DIM), jnp.float32)
    for head in range(heads):
        here = lane == head
        for group in range(1, 2 * SPLIT_TERMS):
            here = here | (lane == head + group * heads)
        left = jnp.where(here, jnp.where(is_maximum, maxima[head], totals[head]), left)
    packed = jnp.zeros_like(left)
    for term in range(SPLIT_TERMS):
        rounded = left.astype(jnp.bfloat16).astype(jnp.float32)
        packed = jnp.where(groups[term] | groups[SPLIT_TERMS + term], rounded, packed)
        left = left - rounded
    return packed.astype(jnp.bfloat16)


def unpack_stats(packed, heads):
    terms = packed.astype(jnp.float32)
    shifted = [terms] + [pltpu.roll(terms, HEAD_DIM - group * heads, 1) for group in range(1, 2 * SPLIT_TERMS)]
    return sum(shifted[1:SPLIT_TERMS], shifted[0]), sum(shifted[SPLIT_TERMS + 1 :], shifted[SPLIT_TERMS])


def attend_kernel(stale_ref, query_parts, key_value_parts, out_refs):
    rows = query_parts[0].shape[0]
    width = query_parts[0].shape[1]
    patch = lax.axis_index("patch")
    uly = lax.axis_index("uly")
    odd = lax.rem(lax.axis_index("rep"), 2)
    key_step = steps_of(0)[KEY] + odd * (steps_of(1)[KEY] - steps_of(0)[KEY])
    heads = range(width // HEAD_DIM)

    def refreshed(kind):
        parts = []
        for block, part_ref in enumerate(key_value_parts):
            home = (patch ^ ((block >> 1) * key_step)) * 2 + (uly ^ (block & 1))
            stale = stale_ref[kind, pl.ds(pl.multiple_of(home * rows, rows), rows), :]
            parts.append(refresh(stale, part_ref[kind * rows : (kind + 1) * rows, :]))
        return jnp.concatenate(parts, axis=0)

    query_rows = jnp.concatenate([part_ref[...] for part_ref in query_parts], axis=0)
    key_rows = refreshed(0)
    scores = [head_scores(query_rows, key_rows, head) for head in heads]
    value_rows = refreshed(1)
    maxima = [jnp.max(each, axis=1, keepdims=True) for each in scores]
    weights = [jnp.exp(each - maximum) for each, maximum in zip(scores, maxima)]
    sums = [weigh_values(weights[head], value_rows, head) for head in heads]
    totals = [jnp.sum(each, axis=1, keepdims=True) for each in weights]
    for head in heads:
        result = (sums[head] / totals[head]).astype(jnp.bfloat16)
        for block, out_ref in enumerate(out_refs):
            out_ref[:, head * HEAD_DIM : (head + 1) * HEAD_DIM] = result[block * rows : (block + 1) * rows]
    stats = pack_stats(maxima, totals)
    for block, out_ref in enumerate(out_refs):
        out_ref[:, width : width + HEAD_DIM] = stats[block * rows : (block + 1) * rows]


def attend_partly(home, home_queries, key_values, other_queries, handed, own_stale):
    rows, width = home_queries.shape

    def body(home_ref, home_queries_ref, *refs):
        named = dict(zip(KEY_VALUE_ORDER, refs))
        other_ref, handed_ref, stale_ref, *out_refs = refs[len(KEY_VALUE_ORDER) :]
        own_columns = aligned(lax.axis_index("uly") * width, width)
        query_parts = (home_queries_ref, handed_ref.at[0], other_ref.at[:, own_columns], handed_ref.at[1])
        attend_kernel(stale_ref, query_parts, (home_ref, *(named[block] for block in (1, 2, 3))), out_refs)

    operands = [home, home_queries, *(key_values[block] for block in KEY_VALUE_ORDER), other_queries, handed, own_stale]
    return kernel_call(body, [(rows, width + HEAD_DIM)] * 4, operands, [pltpu.VMEM] * len(operands))


def merge_side(near_ref, far_ref, out_ref):
    width = near_ref.shape[1] - HEAD_DIM
    heads = width // HEAD_DIM
    near_stats, far_stats = (unpack_stats(ref[:, width:], heads) for ref in (near_ref, far_ref))
    top = jnp.maximum(near_stats[0], far_stats[0])
    near_total = near_stats[1] * jnp.exp(near_stats[0] - top)
    far_total = far_stats[1] * jnp.exp(far_stats[0] - top)
    share = near_total / (near_total + far_total)
    for head in range(heads):
        columns = slice(head * HEAD_DIM, (head + 1) * HEAD_DIM)
        near_rows = near_ref[:, columns].astype(jnp.float32)
        far_rows = far_ref[:, columns].astype(jnp.float32)
        out_ref[:, columns] = (far_rows + (near_rows - far_rows) * share[:, head : head + 1]).astype(jnp.bfloat16)


def merge(parts):
    rows, packed_width = parts[0].shape
    width = packed_width - HEAD_DIM

    def beside_body(far_ref, near_ref, out_ref):
        merge_side(near_ref, far_ref, out_ref)

    (beside,) = kernel_call(beside_body, [(rows, width)], [parts[3], parts[1]], [pltpu.VMEM] * 2)

    def body(beside_ref, near_ref, far_ref, mixed_hbm, own_ref, sems):
        uly = lax.axis_index("uly")
        copies = [
            pltpu.make_async_copy(beside_ref, mixed_hbm.at[:, aligned((1 - uly) * width, width)], sems.at[0]),
            pltpu.make_async_copy(own_ref, mixed_hbm.at[:, aligned(uly * width, width)], sems.at[1]),
        ]
        copies[0].start()
        merge_side(near_ref, far_ref, own_ref)
        copies[1].start()
        for copy in copies:
            copy.wait()

    (mixed,) = kernel_call(
        body,
        [(rows, 2 * width)],
        [beside, parts[0], parts[2]],
        [pltpu.VMEM] * 3,
        [pltpu.VMEM((rows, width), jnp.bfloat16), pltpu.SemaphoreType.DMA((2,))],
        out_space=pltpu.HBM,
    )
    return mixed


def steps_of(rep):
    return (1, 2) if rep % 2 == FAR_QUERY_PARITY else (3, 1)


def swap(array, role, uly):
    peers = lax.axis_size(BOTH)
    pairs = []
    reps = lax.axis_size("rep")
    for rep in range(reps):
        step = 0 if role is None else steps_of(rep)[role]
        pairs += [(peer * reps + rep, (peer ^ (2 * step + uly)) * reps + rep) for peer in range(peers)]
    return lax.ppermute(array, (*BOTH, "rep"), pairs)


def attend_paired(queries, stale_kv, codes, exps):
    half = stale_kv.shape[2]
    other = swap(queries, QUERY, 0)
    away, home, away_queries, home_queries = decode_halves(queries, codes, exps)
    home, stale_kv = lax.optimization_barrier((home, stale_kv))
    own_stale = jnp.swapaxes(stale_kv, 0, 1)
    key_values = {1: swap(away, None, 1), 2: swap(home, KEY, 0), 3: swap(away, KEY, 1)}
    other_away = lax.dynamic_slice(other, (0, (1 - lax.axis_index("uly")) * half), (other.shape[0], half))
    handed = swap(jnp.stack([away_queries, other_away]), None, 1)
    parts = attend_partly(home, home_queries, key_values, other, handed, own_stale)
    homes = ((None, 1), (QUERY, 0), (QUERY, 1))
    return merge([parts[0]] + [swap(part, *home) for part, home in zip(parts[1:], homes)])


def on_device(queries, stale_kv, codes, exps):
    if lax.axis_size("patch") == 4 and lax.axis_size("uly") == 2:
        return attend_paired(queries, stale_kv, codes, exps)
    return attend_gathered(queries, stale_kv, codes, exps)


def solution(mesh):
    return jax.shard_map(
        on_device,
        mesh=mesh,
        in_specs=(
            P(("rep", "patch", "uly"), None),
            P("rep", None, "uly"),
            P(("rep", "patch", "uly"), None, None),
            P(("rep", "patch", "uly"), None, None),
        ),
        out_specs=P(("rep", "patch", "uly"), None),
        check_vma=False,
    )
```

```python
import functools
import math

import jax
import jax.numpy as jnp
from jax import lax
from jax.experimental import pallas as pl
from jax.experimental.pallas import tpu as pltpu
from jax.sharding import PartitionSpec as P

HEAD_DIM = 128
SCALE_BLOCK = 128
KERNEL_VMEM = 8 << 20
BOTH = ("patch", "uly")
SPLIT_TERMS = 3
KEY_VALUE_ORDER = (3, 2, 1)
KEY, QUERY = 0, 1
FAR_QUERY_PARITY = 1


def decode(codes, exps):
    num_rows = codes.shape[0]
    num_blocks = exps.shape[2]
    scaled = (
        codes.astype(jnp.float32).reshape(num_rows, 2, num_blocks, SCALE_BLOCK)
        * jnp.exp2(exps.astype(jnp.float32))[..., None]
    )
    return scaled.reshape(num_rows, 2, num_blocks * SCALE_BLOCK).astype(jnp.bfloat16)


def refresh(stale_part, resid_part):
    return (stale_part.astype(jnp.float32) + resid_part.astype(jnp.float32)).astype(jnp.bfloat16)


def column_block(rows, head):
    return rows[:, head * HEAD_DIM : (head + 1) * HEAD_DIM]


def head_scores(query_rows, key_rows, head):
    scores = lax.dot_general(
        column_block(query_rows, head),
        column_block(key_rows, head),
        (((1,), (1,)), ((), ())),
        preferred_element_type=jnp.float32,
    )
    return scores * (1.0 / math.sqrt(HEAD_DIM))


def weigh_values(weights, value_rows, head):
    return jnp.dot(
        weights.astype(jnp.bfloat16),
        column_block(value_rows, head),
        preferred_element_type=jnp.float32,
    )


def attend_whole(query_rows, kv_rows):
    head_count = query_rows.shape[1] // HEAD_DIM
    key_rows = kv_rows[:, 0]
    value_rows = kv_rows[:, 1]
    outputs = []
    for head in range(head_count):
        scores = head_scores(query_rows, key_rows, head)
        row_max = jnp.max(scores, axis=1, keepdims=True)
        weights = jnp.exp(scores - row_max)
        totals = jnp.sum(weights, axis=1, keepdims=True)
        outputs.append(weigh_values(weights, value_rows, head) / totals)
    return jnp.concatenate(outputs, axis=1).astype(jnp.bfloat16)


def attend_gathered(queries, stale_kv, codes, exps):
    residual = decode(codes, exps)
    query_rows = lax.all_to_all(queries, "uly", split_axis=1, concat_axis=0, tiled=True)
    gathered = lax.all_gather(residual, "patch", axis=0, tiled=True)
    patch_count = lax.axis_size("patch")
    blocked = gathered.reshape(patch_count, residual.shape[0], 2, residual.shape[2])
    spread = lax.all_to_all(blocked, "uly", split_axis=3, concat_axis=1, tiled=True)
    all_resid = spread.reshape(stale_kv.shape)
    result = attend_whole(query_rows, refresh(stale_kv, all_resid))
    return lax.all_to_all(result, "uly", split_axis=0, concat_axis=1, tiled=True)


def aligned(start, size):
    return pl.ds(pl.multiple_of(start, HEAD_DIM), size)


def kernel_call(body, outputs, operands, spaces, scratch=(), out_space=pltpu.VMEM):
    operands = [
        pltpu.with_memory_space_constraint(each, pltpu.HBM) if space is pltpu.HBM else each
        for each, space in zip(operands, spaces)
    ]
    return pl.pallas_call(
        body,
        out_shape=[jax.ShapeDtypeStruct(shape, jnp.bfloat16) for shape in outputs],
        in_specs=[pl.BlockSpec(memory_space=space) for space in spaces],
        out_specs=[pl.BlockSpec(memory_space=out_space)] * len(outputs),
        scratch_shapes=list(scratch),
        compiler_params=pltpu.CompilerParams(vmem_limit_bytes=KERNEL_VMEM),
    )(*operands)


def decode_kernel(
    queries_hbm, codes_hbm, exps_hbm, away_ref, home_ref, away_queries_ref, home_queries_ref, codes_ref, exps_ref, sems
):
    rows, half = home_queries_ref.shape
    uly = lax.axis_index("uly")
    starts = ((1 - uly) * half, uly * half)
    fetch_exps = pltpu.make_async_copy(exps_hbm, exps_ref, sems.at[0])
    fetch_exps.start()
    fetch_codes = []
    for start in starts:
        for kind in range(2):
            slot = len(fetch_codes)
            fetch_codes.append(
                pltpu.make_async_copy(codes_hbm.at[:, kind, aligned(start, half)], codes_ref.at[slot], sems.at[1 + slot])
            )
            fetch_codes[slot].start()
    fetch_queries = []
    for side, target in enumerate((away_queries_ref, home_queries_ref)):
        fetch_queries.append(pltpu.make_async_copy(queries_hbm.at[:, aligned(starts[side], half)], target, sems.at[5 + side]))
        fetch_queries[side].start()
    blocks = exps_ref.shape[2]
    block_of = lax.broadcasted_iota(jnp.int32, (blocks, half), 1) // SCALE_BLOCK
    row_of = lax.broadcasted_iota(jnp.int32, (blocks, half), 0)
    fetch_exps.wait()
    scales = jnp.concatenate([jnp.exp2(exps_ref[:, kind, :].astype(jnp.float32)) for kind in range(2)], axis=0)
    scales = scales.astype(jnp.bfloat16)
    spreads = [(row_of == block_of + start // SCALE_BLOCK).astype(jnp.float32).astype(jnp.bfloat16) for start in starts]
    wide_scales = [jnp.dot(scales, spread, preferred_element_type=jnp.float32) for spread in spreads]
    for side, out_ref in enumerate((away_ref, home_ref)):
        for kind in range(2):
            fetch_codes[2 * side + kind].wait()
            own_rows = slice(kind * rows, (kind + 1) * rows)
            decoded = codes_ref[2 * side + kind].astype(jnp.float32) * wide_scales[side][own_rows]
            out_ref[own_rows, :] = decoded.astype(jnp.bfloat16)
    for fetch in fetch_queries:
        fetch.wait()


def decode_halves(queries, codes, exps):
    rows, model_width = queries.shape
    half = model_width // lax.axis_size("uly")
    return kernel_call(
        decode_kernel,
        [(2 * rows, half)] * 2 + [(rows, half)] * 2,
        [queries, codes, exps],
        [pltpu.HBM] * 3,
        [
            pltpu.VMEM((4, rows, half), codes.dtype),
            pltpu.VMEM(exps.shape, exps.dtype),
            pltpu.SemaphoreType.DMA((7,)),
        ],
    )


def lane_groups(heads):
    lane = lax.broadcasted_iota(jnp.int32, (1, HEAD_DIM), 1)
    return [(lane >= group * heads) & (lane < (group + 1) * heads) for group in range(2 * SPLIT_TERMS)], lane


def pack_stats(maxima, totals):
    heads = len(maxima)
    groups, lane = lane_groups(heads)
    is_maximum = lane < SPLIT_TERMS * heads
    left = jnp.zeros((maxima[0].shape[0], HEAD_DIM), jnp.float32)
    for head in range(heads):
        here = lane == head
        for group in range(1, 2 * SPLIT_TERMS):
            here = here | (lane == head + group * heads)
        left = jnp.where(here, jnp.where(is_maximum, maxima[head], totals[head]), left)
    packed = jnp.zeros_like(left)
    for term in range(SPLIT_TERMS):
        rounded = left.astype(jnp.bfloat16).astype(jnp.float32)
        packed = jnp.where(groups[term] | groups[SPLIT_TERMS + term], rounded, packed)
        left = left - rounded
    return packed.astype(jnp.bfloat16)


def unpack_stats(packed, heads):
    terms = packed.astype(jnp.float32)
    shifted = [terms] + [pltpu.roll(terms, HEAD_DIM - group * heads, 1) for group in range(1, 2 * SPLIT_TERMS)]
    return sum(shifted[1:SPLIT_TERMS], shifted[0]), sum(shifted[SPLIT_TERMS + 1 :], shifted[SPLIT_TERMS])


def attend_kernel(stale_ref, query_parts, key_value_parts, out_refs):
    rows = query_parts[0].shape[0]
    width = query_parts[0].shape[1]
    patch = lax.axis_index("patch")
    uly = lax.axis_index("uly")
    odd = lax.rem(lax.axis_index("rep"), 2)
    key_step = steps_of(0)[KEY] + odd * (steps_of(1)[KEY] - steps_of(0)[KEY])
    heads = range(width // HEAD_DIM)

    def refreshed(kind):
        parts = []
        for block, part_ref in enumerate(key_value_parts):
            home = (patch ^ ((block >> 1) * key_step)) * 2 + (uly ^ (block & 1))
            stale = stale_ref[kind, pl.ds(pl.multiple_of(home * rows, rows), rows), :]
            parts.append(refresh(stale, part_ref[kind * rows : (kind + 1) * rows, :]))
        return jnp.concatenate(parts, axis=0)

    query_rows = jnp.concatenate([part_ref[...] for part_ref in query_parts], axis=0)
    key_rows = refreshed(0)
    scores = [head_scores(query_rows, key_rows, head) for head in heads]
    value_rows = refreshed(1)
    maxima = [jnp.max(each, axis=1, keepdims=True) for each in scores]
    weights = [jnp.exp(each - maximum) for each, maximum in zip(scores, maxima)]
    ones = jnp.ones((value_rows.shape[0], HEAD_DIM), jnp.bfloat16)
    products = []
    for head in heads:
        with_ones = jnp.concatenate([column_block(value_rows, head), ones], axis=1)
        products.append(jnp.dot(weights[head].astype(jnp.bfloat16), with_ones, preferred_element_type=jnp.float32))
    totals = [column_block(each, 1) for each in products]
    for head in heads:
        result = (column_block(products[head], 0) / totals[head]).astype(jnp.bfloat16)
        for block, out_ref in enumerate(out_refs):
            out_ref[:, head * HEAD_DIM : (head + 1) * HEAD_DIM] = result[block * rows : (block + 1) * rows]
    stats = pack_stats(maxima, totals)
    for block, out_ref in enumerate(out_refs):
        out_ref[:, width : width + HEAD_DIM] = stats[block * rows : (block + 1) * rows]


def attend_partly(home, home_queries, key_values, other_queries, handed, own_stale):
    rows, width = home_queries.shape

    def body(home_ref, home_queries_ref, *refs):
        named = dict(zip(KEY_VALUE_ORDER, refs))
        other_ref, handed_ref, stale_ref, *out_refs = refs[len(KEY_VALUE_ORDER) :]
        own_columns = aligned(lax.axis_index("uly") * width, width)
        query_parts = (home_queries_ref, handed_ref.at[0], other_ref.at[:, own_columns], handed_ref.at[1])
        attend_kernel(stale_ref, query_parts, (home_ref, *(named[block] for block in (1, 2, 3))), out_refs)

    operands = [home, home_queries, *(key_values[block] for block in KEY_VALUE_ORDER), other_queries, handed, own_stale]
    return kernel_call(body, [(rows, width + HEAD_DIM)] * 4, operands, [pltpu.VMEM] * len(operands))


def merge_side(near_ref, far_ref, out_ref):
    width = near_ref.shape[1] - HEAD_DIM
    heads = width // HEAD_DIM
    near_stats, far_stats = (unpack_stats(ref[:, width:], heads) for ref in (near_ref, far_ref))
    top = jnp.maximum(near_stats[0], far_stats[0])
    near_total = near_stats[1] * jnp.exp(near_stats[0] - top)
    far_total = far_stats[1] * jnp.exp(far_stats[0] - top)
    share = near_total / (near_total + far_total)
    for head in range(heads):
        columns = slice(head * HEAD_DIM, (head + 1) * HEAD_DIM)
        near_rows = near_ref[:, columns].astype(jnp.float32)
        far_rows = far_ref[:, columns].astype(jnp.float32)
        out_ref[:, columns] = (far_rows + (near_rows - far_rows) * share[:, head : head + 1]).astype(jnp.bfloat16)


def merge(parts):
    rows, packed_width = parts[0].shape
    width = packed_width - HEAD_DIM

    def beside_body(far_ref, near_ref, out_ref):
        merge_side(near_ref, far_ref, out_ref)

    (beside,) = kernel_call(beside_body, [(rows, width)], [parts[3], parts[1]], [pltpu.VMEM] * 2)

    def body(beside_ref, near_ref, far_ref, mixed_hbm, own_ref, sems):
        uly = lax.axis_index("uly")
        copies = [
            pltpu.make_async_copy(beside_ref, mixed_hbm.at[:, aligned((1 - uly) * width, width)], sems.at[0]),
            pltpu.make_async_copy(own_ref, mixed_hbm.at[:, aligned(uly * width, width)], sems.at[1]),
        ]
        copies[0].start()
        merge_side(near_ref, far_ref, own_ref)
        copies[1].start()
        for copy in copies:
            copy.wait()

    (mixed,) = kernel_call(
        body,
        [(rows, 2 * width)],
        [beside, parts[0], parts[2]],
        [pltpu.VMEM] * 3,
        [pltpu.VMEM((rows, width), jnp.bfloat16), pltpu.SemaphoreType.DMA((2,))],
        out_space=pltpu.HBM,
    )
    return mixed


def steps_of(rep):
    return (1, 2) if rep % 2 == FAR_QUERY_PARITY else (3, 1)


def swap(array, role, uly):
    peers = lax.axis_size(BOTH)
    pairs = []
    reps = lax.axis_size("rep")
    for rep in range(reps):
        step = 0 if role is None else steps_of(rep)[role]
        pairs += [(peer * reps + rep, (peer ^ (2 * step + uly)) * reps + rep) for peer in range(peers)]
    return lax.ppermute(array, (*BOTH, "rep"), pairs)


def attend_paired(queries, stale_kv, codes, exps):
    half = stale_kv.shape[2]
    other = swap(queries, QUERY, 0)
    away, home, away_queries, home_queries = decode_halves(queries, codes, exps)
    home, stale_kv = lax.optimization_barrier((home, stale_kv))
    own_stale = jnp.swapaxes(stale_kv, 0, 1)
    key_values = {1: swap(away, None, 1), 2: swap(home, KEY, 0), 3: swap(away, KEY, 1)}
    other_away = lax.dynamic_slice(other, (0, (1 - lax.axis_index("uly")) * half), (other.shape[0], half))
    handed = swap(jnp.stack([away_queries, other_away]), None, 1)
    parts = attend_partly(home, home_queries, key_values, other, handed, own_stale)
    homes = ((None, 1), (QUERY, 0), (QUERY, 1))
    return merge([parts[0]] + [swap(part, *home) for part, home in zip(parts[1:], homes)])


def on_device(queries, stale_kv, codes, exps):
    if lax.axis_size("patch") == 4 and lax.axis_size("uly") == 2:
        return attend_paired(queries, stale_kv, codes, exps)
    return attend_gathered(queries, stale_kv, codes, exps)


def solution(mesh):
    return jax.shard_map(
        on_device,
        mesh=mesh,
        in_specs=(
            P(("rep", "patch", "uly"), None),
            P("rep", None, "uly"),
            P(("rep", "patch", "uly"), None, None),
            P(("rep", "patch", "uly"), None, None),
        ),
        out_specs=P(("rep", "patch", "uly"), None),
        check_vma=False,
    )
```

```python
import functools
import math

import jax
import jax.numpy as jnp
from jax import lax
from jax.experimental import pallas as pl
from jax.experimental.pallas import tpu as pltpu
from jax.sharding import PartitionSpec as P

HEAD_DIM = 128
SCALE_BLOCK = 128
KERNEL_VMEM = 8 << 20
BOTH = ("patch", "uly")
SPLIT_TERMS = 3
KEY_VALUE_ORDER = (3, 2, 1)
KEY, QUERY = 0, 1
FAR_QUERY_PARITY = 1


def decode(codes, exps):
    num_rows = codes.shape[0]
    num_blocks = exps.shape[2]
    scaled = (
        codes.astype(jnp.float32).reshape(num_rows, 2, num_blocks, SCALE_BLOCK)
        * jnp.exp2(exps.astype(jnp.float32))[..., None]
    )
    return scaled.reshape(num_rows, 2, num_blocks * SCALE_BLOCK).astype(jnp.bfloat16)


def refresh(stale_part, resid_part):
    return (stale_part.astype(jnp.float32) + resid_part.astype(jnp.float32)).astype(jnp.bfloat16)


def column_block(rows, head):
    return rows[:, head * HEAD_DIM : (head + 1) * HEAD_DIM]


def head_scores(query_rows, key_rows, head):
    scores = lax.dot_general(
        column_block(query_rows, head),
        column_block(key_rows, head),
        (((1,), (1,)), ((), ())),
        preferred_element_type=jnp.float32,
    )
    return scores * (1.0 / math.sqrt(HEAD_DIM))


def weigh_values(weights, value_rows, head):
    return jnp.dot(
        weights.astype(jnp.bfloat16),
        column_block(value_rows, head),
        preferred_element_type=jnp.float32,
    )


def attend_whole(query_rows, kv_rows):
    head_count = query_rows.shape[1] // HEAD_DIM
    key_rows = kv_rows[:, 0]
    value_rows = kv_rows[:, 1]
    outputs = []
    for head in range(head_count):
        scores = head_scores(query_rows, key_rows, head)
        row_max = jnp.max(scores, axis=1, keepdims=True)
        weights = jnp.exp(scores - row_max)
        totals = jnp.sum(weights, axis=1, keepdims=True)
        outputs.append(weigh_values(weights, value_rows, head) / totals)
    return jnp.concatenate(outputs, axis=1).astype(jnp.bfloat16)


def attend_gathered(queries, stale_kv, codes, exps):
    residual = decode(codes, exps)
    query_rows = lax.all_to_all(queries, "uly", split_axis=1, concat_axis=0, tiled=True)
    gathered = lax.all_gather(residual, "patch", axis=0, tiled=True)
    patch_count = lax.axis_size("patch")
    blocked = gathered.reshape(patch_count, residual.shape[0], 2, residual.shape[2])
    spread = lax.all_to_all(blocked, "uly", split_axis=3, concat_axis=1, tiled=True)
    all_resid = spread.reshape(stale_kv.shape)
    result = attend_whole(query_rows, refresh(stale_kv, all_resid))
    return lax.all_to_all(result, "uly", split_axis=0, concat_axis=1, tiled=True)


def aligned(start, size):
    return pl.ds(pl.multiple_of(start, HEAD_DIM), size)


def kernel_call(body, outputs, operands, spaces, scratch=(), out_space=pltpu.VMEM):
    operands = [
        pltpu.with_memory_space_constraint(each, pltpu.HBM) if space is pltpu.HBM else each
        for each, space in zip(operands, spaces)
    ]
    return pl.pallas_call(
        body,
        out_shape=[jax.ShapeDtypeStruct(shape, jnp.bfloat16) for shape in outputs],
        in_specs=[pl.BlockSpec(memory_space=space) for space in spaces],
        out_specs=[pl.BlockSpec(memory_space=out_space)] * len(outputs),
        scratch_shapes=list(scratch),
        compiler_params=pltpu.CompilerParams(vmem_limit_bytes=KERNEL_VMEM),
    )(*operands)


def decode_kernel(
    queries_hbm, codes_hbm, exps_hbm, away_ref, home_ref, away_queries_ref, home_queries_ref, codes_ref, exps_ref, sems
):
    rows, half = home_queries_ref.shape
    uly = lax.axis_index("uly")
    starts = ((1 - uly) * half, uly * half)
    fetch_exps = pltpu.make_async_copy(exps_hbm, exps_ref, sems.at[0])
    fetch_exps.start()
    fetch_codes = []
    for kind in range(2):
        fetch_codes.append(pltpu.make_async_copy(codes_hbm.at[:, kind, :], codes_ref.at[kind], sems.at[1 + kind]))
        fetch_codes[kind].start()
    fetch_queries = []
    for side, target in enumerate((away_queries_ref, home_queries_ref)):
        fetch_queries.append(pltpu.make_async_copy(queries_hbm.at[:, aligned(starts[side], half)], target, sems.at[5 + side]))
        fetch_queries[side].start()
    blocks = exps_ref.shape[2]
    block_of = lax.broadcasted_iota(jnp.int32, (blocks, half), 1) // SCALE_BLOCK
    row_of = lax.broadcasted_iota(jnp.int32, (blocks, half), 0)
    fetch_exps.wait()
    scales = jnp.concatenate([jnp.exp2(exps_ref[:, kind, :].astype(jnp.float32)) for kind in range(2)], axis=0)
    scales = scales.astype(jnp.bfloat16)
    spreads = [(row_of == block_of + start // SCALE_BLOCK).astype(jnp.float32).astype(jnp.bfloat16) for start in starts]
    wide_scales = [jnp.dot(scales, spread, preferred_element_type=jnp.float32) for spread in spreads]
    for kind in range(2):
        fetch_codes[kind].wait()
        own_rows = slice(kind * rows, (kind + 1) * rows)
        for start, wide_scale, out_ref in zip(starts, wide_scales, (away_ref, home_ref)):
            decoded = codes_ref[kind, :, aligned(start, half)].astype(jnp.float32) * wide_scale[own_rows]
            out_ref[own_rows, :] = decoded.astype(jnp.bfloat16)
    for fetch in fetch_queries:
        fetch.wait()


def decode_halves(queries, codes, exps):
    rows, model_width = queries.shape
    half = model_width // lax.axis_size("uly")
    return kernel_call(
        decode_kernel,
        [(2 * rows, half)] * 2 + [(rows, half)] * 2,
        [queries, codes, exps],
        [pltpu.HBM] * 3,
        [
            pltpu.VMEM((2, rows, model_width), codes.dtype),
            pltpu.VMEM(exps.shape, exps.dtype),
            pltpu.SemaphoreType.DMA((7,)),
        ],
    )


def lane_groups(heads):
    lane = lax.broadcasted_iota(jnp.int32, (1, HEAD_DIM), 1)
    return [(lane >= group * heads) & (lane < (group + 1) * heads) for group in range(2 * SPLIT_TERMS)], lane


def pack_stats(maxima, totals):
    heads = len(maxima)
    groups, lane = lane_groups(heads)
    is_maximum = lane < SPLIT_TERMS * heads
    left = jnp.zeros((maxima[0].shape[0], HEAD_DIM), jnp.float32)
    for head in range(heads):
        here = lane == head
        for group in range(1, 2 * SPLIT_TERMS):
            here = here | (lane == head + group * heads)
        left = jnp.where(here, jnp.where(is_maximum, maxima[head], totals[head]), left)
    packed = jnp.zeros_like(left)
    for term in range(SPLIT_TERMS):
        rounded = left.astype(jnp.bfloat16).astype(jnp.float32)
        packed = jnp.where(groups[term] | groups[SPLIT_TERMS + term], rounded, packed)
        left = left - rounded
    return packed.astype(jnp.bfloat16)


def unpack_stats(packed, heads):
    terms = packed.astype(jnp.float32)
    shifted = [terms] + [pltpu.roll(terms, HEAD_DIM - group * heads, 1) for group in range(1, 2 * SPLIT_TERMS)]
    return sum(shifted[1:SPLIT_TERMS], shifted[0]), sum(shifted[SPLIT_TERMS + 1 :], shifted[SPLIT_TERMS])


def attend_kernel(stale_ref, query_parts, key_value_parts, out_refs):
    rows = query_parts[0].shape[0]
    width = query_parts[0].shape[1]
    patch = lax.axis_index("patch")
    uly = lax.axis_index("uly")
    odd = lax.rem(lax.axis_index("rep"), 2)
    key_step = steps_of(0)[KEY] + odd * (steps_of(1)[KEY] - steps_of(0)[KEY])
    heads = range(width // HEAD_DIM)

    def refreshed(kind):
        parts = []
        for block, part_ref in enumerate(key_value_parts):
            home = (patch ^ ((block >> 1) * key_step)) * 2 + (uly ^ (block & 1))
            stale = stale_ref[kind, pl.ds(pl.multiple_of(home * rows, rows), rows), :]
            parts.append(refresh(stale, part_ref[kind * rows : (kind + 1) * rows, :]))
        return jnp.concatenate(parts, axis=0)

    query_rows = jnp.concatenate([part_ref[...] for part_ref in query_parts], axis=0)
    key_rows = refreshed(0)
    scores = [head_scores(query_rows, key_rows, head) for head in heads]
    value_rows = refreshed(1)
    maxima = [jnp.max(each, axis=1, keepdims=True) for each in scores]
    weights = [jnp.exp(each - maximum) for each, maximum in zip(scores, maxima)]
    ones = jnp.ones((value_rows.shape[0], HEAD_DIM), jnp.bfloat16)
    products = []
    for head in heads:
        with_ones = jnp.concatenate([column_block(value_rows, head), ones], axis=1)
        products.append(jnp.dot(weights[head].astype(jnp.bfloat16), with_ones, preferred_element_type=jnp.float32))
    totals = [column_block(each, 1) for each in products]
    for head in heads:
        result = (column_block(products[head], 0) / totals[head]).astype(jnp.bfloat16)
        for block, out_ref in enumerate(out_refs):
            out_ref[:, head * HEAD_DIM : (head + 1) * HEAD_DIM] = result[block * rows : (block + 1) * rows]
    stats = pack_stats(maxima, totals)
    for block, out_ref in enumerate(out_refs):
        out_ref[:, width : width + HEAD_DIM] = stats[block * rows : (block + 1) * rows]


def attend_partly(home, home_queries, key_values, other_queries, handed, own_stale):
    rows, width = home_queries.shape

    def body(home_ref, home_queries_ref, *refs):
        named = dict(zip(KEY_VALUE_ORDER, refs))
        other_ref, handed_ref, stale_ref, *out_refs = refs[len(KEY_VALUE_ORDER) :]
        own_columns = aligned(lax.axis_index("uly") * width, width)
        query_parts = (home_queries_ref, handed_ref.at[0], other_ref.at[:, own_columns], handed_ref.at[1])
        attend_kernel(stale_ref, query_parts, (home_ref, *(named[block] for block in (1, 2, 3))), out_refs)

    operands = [home, home_queries, *(key_values[block] for block in KEY_VALUE_ORDER), other_queries, handed, own_stale]
    return kernel_call(body, [(rows, width + HEAD_DIM)] * 4, operands, [pltpu.VMEM] * len(operands))


def merge_side(near_ref, far_ref, out_ref):
    width = near_ref.shape[1] - HEAD_DIM
    heads = width // HEAD_DIM
    near_stats, far_stats = (unpack_stats(ref[:, width:], heads) for ref in (near_ref, far_ref))
    top = jnp.maximum(near_stats[0], far_stats[0])
    near_total = near_stats[1] * jnp.exp(near_stats[0] - top)
    far_total = far_stats[1] * jnp.exp(far_stats[0] - top)
    share = near_total / (near_total + far_total)
    for head in range(heads):
        columns = slice(head * HEAD_DIM, (head + 1) * HEAD_DIM)
        near_rows = near_ref[:, columns].astype(jnp.float32)
        far_rows = far_ref[:, columns].astype(jnp.float32)
        out_ref[:, columns] = (far_rows + (near_rows - far_rows) * share[:, head : head + 1]).astype(jnp.bfloat16)


def merge(parts):
    rows, packed_width = parts[0].shape
    width = packed_width - HEAD_DIM

    def beside_body(far_ref, near_ref, out_ref):
        merge_side(near_ref, far_ref, out_ref)

    (beside,) = kernel_call(beside_body, [(rows, width)], [parts[3], parts[1]], [pltpu.VMEM] * 2)

    def body(beside_ref, near_ref, far_ref, mixed_hbm, own_ref, sems):
        uly = lax.axis_index("uly")
        copies = [
            pltpu.make_async_copy(beside_ref, mixed_hbm.at[:, aligned((1 - uly) * width, width)], sems.at[0]),
            pltpu.make_async_copy(own_ref, mixed_hbm.at[:, aligned(uly * width, width)], sems.at[1]),
        ]
        copies[0].start()
        merge_side(near_ref, far_ref, own_ref)
        copies[1].start()
        for copy in copies:
            copy.wait()

    (mixed,) = kernel_call(
        body,
        [(rows, 2 * width)],
        [beside, parts[0], parts[2]],
        [pltpu.VMEM] * 3,
        [pltpu.VMEM((rows, width), jnp.bfloat16), pltpu.SemaphoreType.DMA((2,))],
        out_space=pltpu.HBM,
    )
    return mixed


def steps_of(rep):
    return (1, 2) if rep % 2 == FAR_QUERY_PARITY else (3, 1)


def swap(array, role, uly):
    peers = lax.axis_size(BOTH)
    pairs = []
    reps = lax.axis_size("rep")
    for rep in range(reps):
        step = 0 if role is None else steps_of(rep)[role]
        pairs += [(peer * reps + rep, (peer ^ (2 * step + uly)) * reps + rep) for peer in range(peers)]
    return lax.ppermute(array, (*BOTH, "rep"), pairs)


def attend_paired(queries, stale_kv, codes, exps):
    half = stale_kv.shape[2]
    other = swap(queries, QUERY, 0)
    away, home, away_queries, home_queries = decode_halves(queries, codes, exps)
    home, stale_kv = lax.optimization_barrier((home, stale_kv))
    own_stale = jnp.swapaxes(stale_kv, 0, 1)
    key_values = {1: swap(away, None, 1), 2: swap(home, KEY, 0), 3: swap(away, KEY, 1)}
    other_away = lax.dynamic_slice(other, (0, (1 - lax.axis_index("uly")) * half), (other.shape[0], half))
    handed = swap(jnp.stack([away_queries, other_away]), None, 1)
    parts = attend_partly(home, home_queries, key_values, other, handed, own_stale)
    homes = ((None, 1), (QUERY, 0), (QUERY, 1))
    return merge([parts[0]] + [swap(part, *home) for part, home in zip(parts[1:], homes)])


def on_device(queries, stale_kv, codes, exps):
    if lax.axis_size("patch") == 4 and lax.axis_size("uly") == 2:
        return attend_paired(queries, stale_kv, codes, exps)
    return attend_gathered(queries, stale_kv, codes, exps)


def solution(mesh):
    return jax.shard_map(
        on_device,
        mesh=mesh,
        in_specs=(
            P(("rep", "patch", "uly"), None),
            P("rep", None, "uly"),
            P(("rep", "patch", "uly"), None, None),
            P(("rep", "patch", "uly"), None, None),
        ),
        out_specs=P(("rep", "patch", "uly"), None),
        check_vma=False,
    )
```

```python
import functools
import math

import jax
import jax.numpy as jnp
from jax import lax
from jax.experimental import pallas as pl
from jax.experimental.pallas import tpu as pltpu
from jax.sharding import PartitionSpec as P

HEAD_DIM = 128
SCALE_BLOCK = 128
KERNEL_VMEM = 8 << 20
BOTH = ("patch", "uly")
SPLIT_TERMS = 3
KEY_VALUE_ORDER = (3, 1, 2)
KEY, QUERY = 0, 1
FAR_QUERY_PARITY = 1


def decode(codes, exps):
    num_rows = codes.shape[0]
    num_blocks = exps.shape[2]
    scaled = (
        codes.astype(jnp.float32).reshape(num_rows, 2, num_blocks, SCALE_BLOCK)
        * jnp.exp2(exps.astype(jnp.float32))[..., None]
    )
    return scaled.reshape(num_rows, 2, num_blocks * SCALE_BLOCK).astype(jnp.bfloat16)


def refresh(stale_part, resid_part):
    return (stale_part.astype(jnp.float32) + resid_part.astype(jnp.float32)).astype(jnp.bfloat16)


def column_block(rows, head):
    return rows[:, head * HEAD_DIM : (head + 1) * HEAD_DIM]


def head_scores(query_rows, key_rows, head):
    scores = lax.dot_general(
        column_block(query_rows, head),
        column_block(key_rows, head),
        (((1,), (1,)), ((), ())),
        preferred_element_type=jnp.float32,
    )
    return scores * (1.0 / math.sqrt(HEAD_DIM))


def weigh_values(weights, value_rows, head):
    return jnp.dot(
        weights.astype(jnp.bfloat16),
        column_block(value_rows, head),
        preferred_element_type=jnp.float32,
    )


def attend_whole(query_rows, kv_rows):
    head_count = query_rows.shape[1] // HEAD_DIM
    key_rows = kv_rows[:, 0]
    value_rows = kv_rows[:, 1]
    outputs = []
    for head in range(head_count):
        scores = head_scores(query_rows, key_rows, head)
        row_max = jnp.max(scores, axis=1, keepdims=True)
        weights = jnp.exp(scores - row_max)
        totals = jnp.sum(weights, axis=1, keepdims=True)
        outputs.append(weigh_values(weights, value_rows, head) / totals)
    return jnp.concatenate(outputs, axis=1).astype(jnp.bfloat16)


def attend_gathered(queries, stale_kv, codes, exps):
    residual = decode(codes, exps)
    query_rows = lax.all_to_all(queries, "uly", split_axis=1, concat_axis=0, tiled=True)
    gathered = lax.all_gather(residual, "patch", axis=0, tiled=True)
    patch_count = lax.axis_size("patch")
    blocked = gathered.reshape(patch_count, residual.shape[0], 2, residual.shape[2])
    spread = lax.all_to_all(blocked, "uly", split_axis=3, concat_axis=1, tiled=True)
    all_resid = spread.reshape(stale_kv.shape)
    result = attend_whole(query_rows, refresh(stale_kv, all_resid))
    return lax.all_to_all(result, "uly", split_axis=0, concat_axis=1, tiled=True)


def aligned(start, size):
    return pl.ds(pl.multiple_of(start, HEAD_DIM), size)


def kernel_call(body, outputs, operands, spaces, scratch=(), out_space=pltpu.VMEM):
    operands = [
        pltpu.with_memory_space_constraint(each, pltpu.HBM) if space is pltpu.HBM else each
        for each, space in zip(operands, spaces)
    ]
    return pl.pallas_call(
        body,
        out_shape=[jax.ShapeDtypeStruct(shape, jnp.bfloat16) for shape in outputs],
        in_specs=[pl.BlockSpec(memory_space=space) for space in spaces],
        out_specs=[pl.BlockSpec(memory_space=out_space)] * len(outputs),
        scratch_shapes=list(scratch),
        compiler_params=pltpu.CompilerParams(vmem_limit_bytes=KERNEL_VMEM),
    )(*operands)


def decode_kernel(
    queries_hbm, codes_hbm, exps_hbm, away_ref, home_ref, away_queries_ref, home_queries_ref, codes_ref, exps_ref, sems
):
    rows, half = home_queries_ref.shape
    uly = lax.axis_index("uly")
    starts = ((1 - uly) * half, uly * half)
    fetch_exps = pltpu.make_async_copy(exps_hbm, exps_ref, sems.at[0])
    fetch_exps.start()
    fetch_codes = []
    for start in starts:
        for kind in range(2):
            slot = len(fetch_codes)
            fetch_codes.append(
                pltpu.make_async_copy(codes_hbm.at[:, kind, aligned(start, half)], codes_ref.at[slot], sems.at[1 + slot])
            )
            fetch_codes[slot].start()
    fetch_queries = []
    for side, target in enumerate((away_queries_ref, home_queries_ref)):
        fetch_queries.append(pltpu.make_async_copy(queries_hbm.at[:, aligned(starts[side], half)], target, sems.at[5 + side]))
        fetch_queries[side].start()
    blocks = exps_ref.shape[2]
    block_of = lax.broadcasted_iota(jnp.int32, (blocks, half), 1) // SCALE_BLOCK
    row_of = lax.broadcasted_iota(jnp.int32, (blocks, half), 0)
    fetch_exps.wait()
    scales = jnp.concatenate([jnp.exp2(exps_ref[:, kind, :].astype(jnp.float32)) for kind in range(2)], axis=0)
    scales = scales.astype(jnp.bfloat16)
    spreads = [(row_of == block_of + start // SCALE_BLOCK).astype(jnp.float32).astype(jnp.bfloat16) for start in starts]
    wide_scales = [jnp.dot(scales, spread, preferred_element_type=jnp.float32) for spread in spreads]
    for side, out_ref in enumerate((away_ref, home_ref)):
        for kind in range(2):
            fetch_codes[2 * side + kind].wait()
            own_rows = slice(kind * rows, (kind + 1) * rows)
            decoded = codes_ref[2 * side + kind].astype(jnp.float32) * wide_scales[side][own_rows]
            out_ref[own_rows, :] = decoded.astype(jnp.bfloat16)
    for fetch in fetch_queries:
        fetch.wait()


def decode_halves(queries, codes, exps):
    rows, model_width = queries.shape
    half = model_width // lax.axis_size("uly")
    return kernel_call(
        decode_kernel,
        [(2 * rows, half)] * 2 + [(rows, half)] * 2,
        [queries, codes, exps],
        [pltpu.HBM] * 3,
        [
            pltpu.VMEM((4, rows, half), codes.dtype),
            pltpu.VMEM(exps.shape, exps.dtype),
            pltpu.SemaphoreType.DMA((7,)),
        ],
    )


def lane_groups(heads):
    lane = lax.broadcasted_iota(jnp.int32, (1, HEAD_DIM), 1)
    return [(lane >= group * heads) & (lane < (group + 1) * heads) for group in range(2 * SPLIT_TERMS)], lane


def pack_stats(maxima, totals):
    heads = len(maxima)
    groups, lane = lane_groups(heads)
    is_maximum = lane < SPLIT_TERMS * heads
    left = jnp.zeros((maxima[0].shape[0], HEAD_DIM), jnp.float32)
    for head in range(heads):
        here = lane == head
        for group in range(1, 2 * SPLIT_TERMS):
            here = here | (lane == head + group * heads)
        left = jnp.where(here, jnp.where(is_maximum, maxima[head], totals[head]), left)
    packed = jnp.zeros_like(left)
    for term in range(SPLIT_TERMS):
        rounded = left.astype(jnp.bfloat16).astype(jnp.float32)
        packed = jnp.where(groups[term] | groups[SPLIT_TERMS + term], rounded, packed)
        left = left - rounded
    return packed.astype(jnp.bfloat16)


def unpack_stats(packed, heads):
    terms = packed.astype(jnp.float32)
    shifted = [terms] + [pltpu.roll(terms, HEAD_DIM - group * heads, 1) for group in range(1, 2 * SPLIT_TERMS)]
    return sum(shifted[1:SPLIT_TERMS], shifted[0]), sum(shifted[SPLIT_TERMS + 1 :], shifted[SPLIT_TERMS])


def attend_kernel(stale_ref, query_parts, key_value_parts, out_refs):
    rows = query_parts[0].shape[0]
    width = query_parts[0].shape[1]
    patch = lax.axis_index("patch")
    uly = lax.axis_index("uly")
    odd = lax.rem(lax.axis_index("rep"), 2)
    key_step = steps_of(0)[KEY] + odd * (steps_of(1)[KEY] - steps_of(0)[KEY])
    heads = range(width // HEAD_DIM)

    def refreshed(kind):
        parts = []
        for block, part_ref in enumerate(key_value_parts):
            home = (patch ^ ((block >> 1) * key_step)) * 2 + (uly ^ (block & 1))
            stale = stale_ref[kind, pl.ds(pl.multiple_of(home * rows, rows), rows), :]
            parts.append(refresh(stale, part_ref[kind * rows : (kind + 1) * rows, :]))
        return jnp.concatenate(parts, axis=0)

    query_rows = jnp.concatenate([part_ref[...] for part_ref in query_parts], axis=0)
    key_rows = refreshed(0)
    scores = [head_scores(query_rows, key_rows, head) for head in heads]
    value_rows = refreshed(1)
    maxima = [jnp.max(each, axis=1, keepdims=True) for each in scores]
    weights = [jnp.exp(each - maximum) for each, maximum in zip(scores, maxima)]
    sums = [weigh_values(weights[head], value_rows, head) for head in heads]
    totals = [jnp.sum(each, axis=1, keepdims=True) for each in weights]
    for head in heads:
        result = (sums[head] / totals[head]).astype(jnp.bfloat16)
        for block, out_ref in enumerate(out_refs):
            out_ref[:, head * HEAD_DIM : (head + 1) * HEAD_DIM] = result[block * rows : (block + 1) * rows]
    stats = pack_stats(maxima, totals)
    for block, out_ref in enumerate(out_refs):
        out_ref[:, width : width + HEAD_DIM] = stats[block * rows : (block + 1) * rows]


def attend_partly(home, home_queries, key_values, other_queries, handed, own_stale):
    rows, width = home_queries.shape

    def body(home_ref, home_queries_ref, *refs):
        named = dict(zip(KEY_VALUE_ORDER, refs))
        other_ref, handed_ref, stale_ref, *out_refs = refs[len(KEY_VALUE_ORDER) :]
        own_columns = aligned(lax.axis_index("uly") * width, width)
        query_parts = (home_queries_ref, handed_ref.at[0], other_ref.at[:, own_columns], handed_ref.at[1])
        attend_kernel(stale_ref, query_parts, (home_ref, *(named[block] for block in (1, 2, 3))), out_refs)

    operands = [home, home_queries, *(key_values[block] for block in KEY_VALUE_ORDER), other_queries, handed, own_stale]
    return kernel_call(body, [(rows, width + HEAD_DIM)] * 4, operands, [pltpu.VMEM] * len(operands))


def merge_side(near_ref, far_ref, out_ref):
    width = near_ref.shape[1] - HEAD_DIM
    heads = width // HEAD_DIM
    near_stats, far_stats = (unpack_stats(ref[:, width:], heads) for ref in (near_ref, far_ref))
    top = jnp.maximum(near_stats[0], far_stats[0])
    near_total = near_stats[1] * jnp.exp(near_stats[0] - top)
    far_total = far_stats[1] * jnp.exp(far_stats[0] - top)
    share = near_total / (near_total + far_total)
    for head in range(heads):
        columns = slice(head * HEAD_DIM, (head + 1) * HEAD_DIM)
        near_rows = near_ref[:, columns].astype(jnp.float32)
        far_rows = far_ref[:, columns].astype(jnp.float32)
        out_ref[:, columns] = (far_rows + (near_rows - far_rows) * share[:, head : head + 1]).astype(jnp.bfloat16)


def merge(parts):
    rows, packed_width = parts[0].shape
    width = packed_width - HEAD_DIM

    def beside_body(far_ref, near_ref, out_ref):
        merge_side(near_ref, far_ref, out_ref)

    (beside,) = kernel_call(beside_body, [(rows, width)], [parts[3], parts[1]], [pltpu.VMEM] * 2)

    def body(beside_ref, near_ref, far_ref, mixed_hbm, own_ref, sems):
        uly = lax.axis_index("uly")
        copies = [
            pltpu.make_async_copy(beside_ref, mixed_hbm.at[:, aligned((1 - uly) * width, width)], sems.at[0]),
            pltpu.make_async_copy(own_ref, mixed_hbm.at[:, aligned(uly * width, width)], sems.at[1]),
        ]
        copies[0].start()
        merge_side(near_ref, far_ref, own_ref)
        copies[1].start()
        for copy in copies:
            copy.wait()

    (mixed,) = kernel_call(
        body,
        [(rows, 2 * width)],
        [beside, parts[0], parts[2]],
        [pltpu.VMEM] * 3,
        [pltpu.VMEM((rows, width), jnp.bfloat16), pltpu.SemaphoreType.DMA((2,))],
        out_space=pltpu.HBM,
    )
    return mixed


def steps_of(rep):
    return (1, 2) if rep % 2 == FAR_QUERY_PARITY else (3, 1)


def swap(array, role, uly):
    peers = lax.axis_size(BOTH)
    pairs = []
    reps = lax.axis_size("rep")
    for rep in range(reps):
        step = 0 if role is None else steps_of(rep)[role]
        pairs += [(peer * reps + rep, (peer ^ (2 * step + uly)) * reps + rep) for peer in range(peers)]
    return lax.ppermute(array, (*BOTH, "rep"), pairs)


def attend_paired(queries, stale_kv, codes, exps):
    half = stale_kv.shape[2]
    other = swap(queries, QUERY, 0)
    away, home, away_queries, home_queries = decode_halves(queries, codes, exps)
    home, stale_kv = lax.optimization_barrier((home, stale_kv))
    own_stale = jnp.swapaxes(stale_kv, 0, 1)
    key_values = {1: swap(away, None, 1), 2: swap(home, KEY, 0), 3: swap(away, KEY, 1)}
    other_away = lax.dynamic_slice(other, (0, (1 - lax.axis_index("uly")) * half), (other.shape[0], half))
    handed = swap(jnp.stack([away_queries, other_away]), None, 1)
    parts = attend_partly(home, home_queries, key_values, other, handed, own_stale)
    homes = ((None, 1), (QUERY, 0), (QUERY, 1))
    return merge([parts[0]] + [swap(part, *home) for part, home in zip(parts[1:], homes)])


def on_device(queries, stale_kv, codes, exps):
    if lax.axis_size("patch") == 4 and lax.axis_size("uly") == 2:
        return attend_paired(queries, stale_kv, codes, exps)
    return attend_gathered(queries, stale_kv, codes, exps)


def solution(mesh):
    return jax.shard_map(
        on_device,
        mesh=mesh,
        in_specs=(
            P(("rep", "patch", "uly"), None),
            P("rep", None, "uly"),
            P(("rep", "patch", "uly"), None, None),
            P(("rep", "patch", "uly"), None, None),
        ),
        out_specs=P(("rep", "patch", "uly"), None),
        check_vma=False,
    )
```
